32 devices in a mesh: groups: 1, ep: 32 (over z, y, x, core).
Axes of the slice: x: 2, y: 2, z: 4, core: 2. Of those that a mesh axis runs over, the one named last changes fastest.
Arguments:
- tokens: bfloat16 [2, 256, 3584], P(None, ('groups', 'ep')), may hold values from -6 to 6
- expert_ids: int32 [2, 256, 8], P(None, ('groups', 'ep')), may hold values from 0 to 15, all different within a row; in each aligned block of 8 rows (0 to 7, 8 to 15, ..., all dimensions but the last counted through in order) at most 8 rows name the same one
- route_weight: float32 [2, 256, 8], P(None, ('groups', 'ep')), may hold values from 0.05 to 1
- gate_weight: bfloat16 [32, 3584, 512], P('ep'), may hold values from -0.09375 to 0.09375
- up_weight: bfloat16 [32, 3584, 512], P('ep'), may hold values from -0.09375 to 0.09375
- down_weight: bfloat16 [32, 512, 3584], P('ep'), may hold values from -0.1875 to 0.1875
Outputs:
- combined: bfloat16 [2, 256, 3584], P(None, ('groups', 'ep'))
The draws below stay inside these ranges and needn't reach their ends.
Inputs may be any that keep to these rules, and one draw needn't show every extreme that they name: `expert_ids`: each row names 8 different experts; within each step, the 8 rows of one device name any one expert at most 8 times.
All inputs are finite; a program needn't handle non-finite values.
Results may differ from the reference program's by a relative error of at most 0.0065.
Values may be sent and summed in bfloat16 or wider, within the bound.
A program may use at most 64 MiB of HBM per device.

```python
import math
import jax
import jax.numpy as jnp
import numpy as np
from jax import lax

D_WIN = 3584
FF_WIN = 1024
TOP = 8
STEPS = 2
TOK_DEV = 8
EXPERTS = 16
CAP = 8
TOKENS = 256
N_EP = 32


def levels(rng, dims, pieces, least, top_value):
    factor_of, own = 1.0, jax.random.fold_in(rng, 6)
    for axis_at, shards_of in pieces:
        draws = jnp.exp(jax.random.uniform(jax.random.fold_in(own, axis_at), (shards_of,), jnp.float32, least / len(pieces), top_value / len(pieces)))
        factor_of = factor_of * jnp.repeat(draws, dims[axis_at] // shards_of).reshape([-1 if axis == axis_at else 1 for axis in range(len(dims))])
    return factor_of


def assign_block(stream_key, own, number, rows, number_of, top, reach, skew):
    ranking = jax.random.permutation(stream_key, number_of)
    heavy_load, usual = portions_of(number_of, rows * top, reach, skew, True), portions_of(number_of, rows * top, reach, skew, False)
    places = jnp.arange(number_of)

    def named(lengths, rotation):
        used = int((lengths > 0).sum())
        fixed = max(1, used // 4)
        shifted = fixed + (places - fixed + rotation * (used - fixed)) % max(1, number_of - fixed)
        return jnp.zeros((number_of,), jnp.int32).at[ranking[jnp.where(places < fixed, places, shifted)]].set(jnp.asarray(lengths, jnp.int32))

    lengths = jnp.where(number % 4 == 0, named(heavy_load, number // 4), named(usual, number - number // 4 - 1))
    mixed = jax.random.permutation(jax.random.fold_in(own, 3), number_of)
    source_of, sink = mixed[0:number_of // 2 * 2:2], mixed[1:number_of // 2 * 2:2]
    room = jnp.minimum(lengths[source_of] - 1, reach - lengths[sink]) // 2
    room = jnp.where((source_of == ranking[0]) | (sink == ranking[0]) | (lengths[sink] == 0), 0, jnp.maximum(room, 0))
    shifted = jax.random.randint(jax.random.fold_in(own, 4), (number_of // 2,), 0, 1 << 20) % (room + 1)
    lengths = lengths.at[source_of].add(-shifted).at[sink].add(shifted)
    members = jnp.searchsorted(jnp.cumsum(lengths), jnp.arange(rows * top), side="right").astype(jnp.int32)
    listing = members.reshape(top, rows).T
    listing = listing[jax.random.permutation(jax.random.fold_in(own, 1), rows)]
    rotation = jax.random.randint(jax.random.fold_in(own, 2), (rows, 1), 0, top)
    return jnp.take_along_axis(listing, (jnp.arange(top)[None, :] + rotation) % top, axis=1)


def portions_of(number_of, total, bound, skew, full):
    portions = [(1 << 20) // math.isqrt(grade ** skew) + 1 for grade in range(1, number_of + 1)]
    largest = bound if full else min(bound, max(-(-total // number_of), total * portions[0] // sum(portions)))
    least = 1 if total - largest >= number_of - 1 else 0
    holding, spare = [largest] + [least] * (number_of - 1), total - largest - least * (number_of - 1)
    while spare > 0:
        free = [i for i in range(1, number_of) if holding[i] < largest] or [i for i in range(1, number_of) if holding[i] < bound]
        mass, left = sum([portions[i] for i in free]), spare
        for i in free:
            extra = min(bound - holding[i], max(1, left * portions[i] // mass), spare)
            holding[i] = holding[i] + extra
            spare = spare - extra
    return np.array(holding)


def centred(key, shape, scale, reach, pieces=(), kind=jnp.bfloat16):
    values = jax.random.normal(key, shape, jnp.float32) * scale
    if len(pieces) > 0:
        values = levels(key, shape, pieces, -0.22, 0.18) * values
    return jnp.clip(values, min=-reach, max=reach).astype(kind)


def setup_inputs(seed: int = 0, part: int = 0) -> dict:
    splits = jax.random.split(jax.random.key(seed), 7)
    part_keys = jax.random.split(jax.random.fold_in(splits[6], part), 7)
    tokens = centred(part_keys[0], (STEPS, TOKENS, D_WIN), 1.0, 6.0, ((1, 32),))
    expert_ids_keys = jax.random.split(jax.random.fold_in(part_keys[1], 1), STEPS * TOKENS // TOK_DEV)
    expert_ids_turns = jax.random.permutation(jax.random.fold_in(part_keys[1], 3), STEPS * TOKENS // TOK_DEV)
    expert_ids = jax.vmap(lambda own, number: assign_block(jax.random.fold_in(part_keys[1], 2), own, number, TOK_DEV, EXPERTS, TOP, CAP, 2))(expert_ids_keys, expert_ids_turns).reshape((STEPS, TOKENS, TOP))
    route_weight = jnp.clip(jnp.exp(math.log(1.0) - 2.9957323 * jax.random.uniform(part_keys[2], (STEPS, TOKENS, TOP), jnp.float32) ** levels(part_keys[2], (STEPS, TOKENS, TOP), ((1, 32),), -0.2, 0.2)), 0.05, 1.0)
    gate_weight = centred(splits[3], (N_EP, D_WIN, FF_WIN // 2), D_WIN ** -0.5, 0.09375, ((0, 32),))
    up_weight = centred(splits[4], (N_EP, D_WIN, FF_WIN // 2), D_WIN ** -0.5, 0.09375, ((0, 32),))
    down_weight = centred(splits[5], (N_EP, FF_WIN // 2, D_WIN), FF_WIN ** -0.5, 0.1875, ((0, 32),))
    return {"tokens": tokens, "expert_ids": expert_ids, "route_weight": route_weight, "gate_weight": gate_weight, "up_weight": up_weight, "down_weight": down_weight}


def slot_layout(block_ids, expert_count, capacity):
    pairs = block_ids.reshape(-1).astype(jnp.int32)
    count = pairs.shape[0]
    one_hot = (pairs[:, None] == jnp.arange(expert_count, dtype=jnp.int32)[None, :]).astype(jnp.float32)
    order = jnp.arange(count, dtype=jnp.int32)
    earlier = (order[None, :] < order[:, None]).astype(jnp.float32)
    before = jnp.dot(earlier, one_hot, precision=lax.Precision.HIGHEST)
    slot_rank = jnp.sum(before * one_hot, axis=1).astype(jnp.int32)
    slot_index = pairs * capacity + slot_rank
    slot_source = jnp.full((expert_count * capacity,), count, jnp.int32).at[slot_index].set(order)
    return slot_index, slot_source


def reference(tokens, expert_ids, route_weight, gate_weight, up_weight, down_weight):
    half_units = FF_WIN // 2
    gates = gate_weight.reshape(EXPERTS, 2, D_WIN, half_units)
    ups = up_weight.reshape(EXPERTS, 2, D_WIN, half_units)
    downs = down_weight.reshape(EXPERTS, 2, half_units, D_WIN)
    outputs = []
    for step_index in range(STEPS):
        inputs = tokens[step_index]
        block_ids = expert_ids[step_index].reshape(N_EP, TOK_DEV, TOP)
        slot_index, slot_source = jax.vmap(lambda blk: slot_layout(blk, EXPERTS, CAP))(block_ids)
        local_row = (slot_source // TOP).astype(jnp.int32)
        unused = local_row == TOK_DEV
        offsets = (TOK_DEV * jnp.arange(N_EP, dtype=jnp.int32))[:, None]
        global_row = jnp.where(unused, jnp.int32(TOKENS), local_row + offsets).astype(jnp.int32)
        gathers = global_row.reshape(N_EP, EXPERTS, CAP).transpose(1, 0, 2).reshape(EXPERTS, N_EP * CAP)
        padded = jnp.concatenate([inputs, jnp.zeros((1, D_WIN), inputs.dtype)], axis=0)

        def apply_expert(operands):
            gate_m, up_m, down_m, rows_index = operands
            rows = padded[rows_index]
            total = jnp.zeros((rows.shape[0], D_WIN), jnp.float32)
            for half in range(2):
                gate = jnp.dot(rows, gate_m[half], preferred_element_type=jnp.float32)
                upper = jnp.dot(rows, up_m[half], preferred_element_type=jnp.float32)
                act = (jax.nn.silu(gate) * upper).astype(jnp.bfloat16)
                part = jnp.dot(act, down_m[half], preferred_element_type=jnp.float32).astype(jnp.bfloat16)
                total = total + part.astype(jnp.float32)
            return total.astype(jnp.bfloat16)

        results = lax.map(apply_expert, (gates, ups, downs, gathers))
        expert_of = slot_index // CAP
        slot_rank = slot_index % CAP
        sources = jnp.arange(N_EP, dtype=jnp.int32)[:, None]
        positions = (expert_of * (N_EP * CAP) + sources * CAP + slot_rank).astype(jnp.int32)
        picked = results.reshape(-1, D_WIN)[positions.reshape(-1)].reshape(TOKENS, TOP, D_WIN)
        summed = jnp.sum(route_weight[step_index][:, :, None] * picked.astype(jnp.float32), axis=1)
        outputs.append(summed.astype(jnp.bfloat16))
    return jnp.stack(outputs)
```

```python
import jax
import jax.numpy as jnp
from jax import lax
from jax.sharding import PartitionSpec as P

TOP = 8
STEPS = 2


def partner_2(block, axis, apart):
    count = lax.axis_size(axis)
    route = []
    for low in range(count):
        high = low | 1 << apart
        if high != low and high < count:
            route += [(low, high), (high, low)]
    return lax.ppermute(block, axis, route)


def slot_layout(block_ids, expert_count, capacity):
    pairs = block_ids.reshape(-1)
    count = pairs.shape[0]
    one_hot = (pairs[:, None] == jnp.arange(expert_count, dtype=jnp.int32)[None, :]).astype(
        jnp.float32
    )
    order = jnp.arange(count, dtype=jnp.int32)
    earlier = (order[None, :] < order[:, None]).astype(jnp.float32)
    before = jnp.dot(earlier, one_hot, precision=lax.Precision.HIGHEST)
    slot_rank = jnp.sum(before * one_hot, axis=1).astype(jnp.int32)
    slot_index = pairs * capacity + slot_rank
    slot_source = jnp.full((expert_count * capacity,), count, jnp.int32).at[slot_index].set(order)
    return (slot_index, slot_source)


def dense(tokens, expert_ids, route_weight, gate_weight, up_weight, down_weight):
    expert_count = lax.axis_size("ep") // 2
    named = expert_ids[..., None] == jnp.arange(expert_count, dtype=jnp.int32)
    coef = jnp.sum(jnp.where(named, route_weight[..., None], 0.0), axis=2)
    coefs = lax.all_gather(coef, "ep", axis=1, tiled=True)
    rows = lax.all_gather(tokens, "ep", axis=1, tiled=True)
    mine = lax.dynamic_index_in_dim(coefs, lax.axis_index("ep") // 2, axis=2, keepdims=True)
    gate = jnp.einsum("std,df->stf", rows, gate_weight[0], preferred_element_type=jnp.float32)
    upper = jnp.einsum("std,df->stf", rows, up_weight[0], preferred_element_type=jnp.float32)
    act = (mine * (jax.nn.silu(gate) * upper)).astype(jnp.bfloat16)
    part = jnp.einsum("stf,fd->std", act, down_weight[0], preferred_element_type=jnp.float32)
    return lax.psum_scatter(part.astype(jnp.bfloat16), "ep", scatter_dimension=1, tiled=True)


def shards(tokens, expert_ids, route_weight, gate_weight, up_weight, down_weight):
    device_count = lax.axis_size("ep")
    expert_count = device_count // 2
    tok_rows = tokens.shape[1]
    features = tokens.shape[2]
    capacity = min(tok_rows, 2 * tok_rows * TOP // expert_count)
    if capacity == tok_rows:
        return dense(tokens, expert_ids, route_weight, gate_weight, up_weight, down_weight)
    half_slots = capacity // 2
    gate_m = gate_weight[0]
    up_m = up_weight[0]
    down_m = down_weight[0]
    parity_odd = lax.axis_index("ep") % 2 == 1
    layouts = []
    outgoing = []
    for step_index in range(STEPS):
        slot_index, slot_source = slot_layout(expert_ids[step_index], expert_count, capacity)
        padded = jnp.concatenate(
            [tokens[step_index], jnp.zeros((1, features), tokens.dtype)], axis=0
        )
        blocks = padded[slot_source // TOP].reshape(expert_count, capacity, features)
        arrange_paired = blocks.reshape(expert_count, half_slots, 2, features)
        arrange_paired = jnp.where(parity_odd, arrange_paired[:, :, ::-1], arrange_paired)
        outgoing.append(
            arrange_paired.transpose(0, 2, 1, 3).reshape(device_count, half_slots, features)
        )
        layouts.append(slot_index)
    returned_list = []
    for sent in outgoing:
        received = lax.all_to_all(sent, "ep", split_axis=0, concat_axis=0, tiled=True)
        partner = partner_2(received, "ep", 0)
        width = received.shape[1]
        apply_received = jnp.concatenate([received, partner], axis=1)
        gate = jnp.einsum("scd,df->scf", apply_received, gate_m, preferred_element_type=jnp.float32)
        upper = jnp.einsum("scd,df->scf", apply_received, up_m, preferred_element_type=jnp.float32)
        act = (jax.nn.silu(gate) * upper).astype(jnp.bfloat16)
        parts = jnp.einsum("scf,fd->scd", act, down_m, preferred_element_type=jnp.float32).astype(
            jnp.bfloat16
        )
        back = partner_2(parts[:, width:], "ep", 0)
        summed = (parts[:, :width].astype(jnp.float32) + back.astype(jnp.float32)).astype(
            jnp.bfloat16
        )
        returned_list.append(lax.all_to_all(summed, "ep", split_axis=0, concat_axis=0, tiled=True))
    answers = []
    for step_index in range(STEPS):
        returned = returned_list[step_index]
        paired = returned.reshape(expert_count, 2, half_slots, features).transpose(0, 2, 1, 3)
        paired = jnp.where(parity_odd, paired[:, :, ::-1], paired)
        answers.append(paired.reshape(expert_count, capacity, features))
    outputs = []
    for step_index in range(STEPS):
        flattened = answers[step_index].reshape(expert_count * capacity, features)
        picked = flattened[layouts[step_index]].reshape(tok_rows, TOP, features)
        summed = jnp.sum(route_weight[step_index][:, :, None] * picked.astype(jnp.float32), axis=1)
        outputs.append(summed.astype(jnp.bfloat16))
    return jnp.stack(outputs)


def solution(mesh):
    in_specs = (
        P(None, ("groups", "ep"), None),
        P(None, ("groups", "ep"), None),
        P(None, ("groups", "ep"), None),
        P("ep", None, None),
        P("ep", None, None),
        P("ep", None, None),
    )
    out_specs = P(None, ("groups", "ep"), None)
    return jax.shard_map(shards, mesh=mesh, in_specs=in_specs, out_specs=out_specs, check_vma=False)
```

```python
import functools

import jax
import jax.numpy as jnp
from jax import lax
from jax.experimental import pallas as pl
from jax.experimental.pallas import tpu as pltpu
from jax.sharding import PartitionSpec as P

TOP = 8
STEPS = 2


def partner_2(block, axis, apart):
    count = lax.axis_size(axis)
    route = []
    for low in range(count):
        high = low | 1 << apart
        if high != low and high < count:
            route += [(low, high), (high, low)]
    return lax.ppermute(block, axis, route)


def slot_layout(block_ids, expert_count, capacity):
    pairs = block_ids.reshape(-1)
    count = pairs.shape[0]
    one_hot = (pairs[:, None] == jnp.arange(expert_count, dtype=jnp.int32)[None, :]).astype(
        jnp.float32
    )
    order = jnp.arange(count, dtype=jnp.int32)
    earlier = (order[None, :] < order[:, None]).astype(jnp.float32)
    before = jnp.dot(earlier, one_hot, precision=lax.Precision.HIGHEST)
    slot_rank = jnp.sum(before * one_hot, axis=1).astype(jnp.int32)
    slot_index = pairs * capacity + slot_rank
    slot_source = jnp.full((expert_count * capacity,), count, jnp.int32).at[slot_index].set(order)
    return (slot_index, slot_source)


LANES = 128
SQUARE = 4
CORES = 2
FF_TILE = 256
OUT_TILE = 512


def peer_at(k, z, nz):
    low = lax.div(2 * (nz - 1 - z) + 1, nz)
    at = z * low + (nz - 1 - z) * (1 - low)
    other = k + lax.div(k - at + nz, nz)
    return other * low + (nz - 1 - other) * (1 - low)


def fused_kernel(
    nz, tok_ref, ids_ref, route_ref, gate_hbm, up_hbm, down_hbm, out_ref,
    gate_w, up_w, down_w, xg, act, part, rs, r1, r2, rz,
    w_sem, x_recv, x_send_z, x_send_a, x_send_b, x_send_s,
    rs_send, rs_recv, r1_send, r1_recv, r2_send, r2_recv, rz_send, rz_recv,
):
    steps, tok_rows, features = tok_ref.shape
    rows = steps * tok_rows
    hidden = act.shape[1]
    experts = nz * SQUARE
    me = lax.axis_index("ep")
    c = lax.rem(me, CORES)
    expert = lax.div(me, CORES)
    q = lax.rem(expert, SQUARE)
    z = lax.div(expert, SQUARE)
    x, y = lax.rem(q, 2), lax.div(q, 2)
    qx, qy = 2 * y + 1 - x, 2 * (1 - y) + x
    qa = qx * (1 - c) + qy * c
    qb = qy * (1 - c) + qx * c
    qd = 3 - q
    s = 1 - c

    def device(to_z, to_q, to_c):
        return {"ep": (to_z * SQUARE + to_q) * CORES + to_c}

    sibling, along_a, along_b = device(z, q, s), device(z, qa, c), device(z, qb, c)
    peers = [peer_at(k, z, nz) for k in range(nz - 1)]
    near = [z] + peers

    loads = [
        pltpu.make_async_copy(gate_hbm.at[0], gate_w, w_sem.at[0]),
        pltpu.make_async_copy(up_hbm.at[0], up_w, w_sem.at[1]),
        pltpu.make_async_copy(down_hbm.at[0], down_w, w_sem.at[2]),
    ]
    barrier = pltpu.get_barrier_semaphore()
    partners = [device(p, q, c) for p in peers] + [along_a, along_b, sibling]
    for partner in partners:
        pl.semaphore_signal(
            barrier, inc=1, device_id=partner, device_id_type=pl.DeviceIdType.MESH
        )
    for load in loads:
        load.start()

    xg[q, c, z, :, :features] = (
        tok_ref[...].astype(jnp.float32).reshape(rows, features).astype(jnp.bfloat16)
    )
    lane = lax.broadcasted_iota(jnp.int32, (rows, LANES), 1)
    lane_expert, lane_piece = lax.rem(lane, experts), lax.div(lane, experts)
    ids = ids_ref[...].reshape(rows, TOP)
    route = route_ref[...].reshape(rows, TOP)
    coef = jnp.zeros((rows, LANES), jnp.float32)
    for k in range(TOP):
        coef += jnp.where(ids[:, k : k + 1] == lane_expert, route[:, k : k + 1], 0.0)
    high = coef.astype(jnp.bfloat16).astype(jnp.float32)
    middle = (coef - high).astype(jnp.bfloat16).astype(jnp.float32)
    low = coef - high - middle
    pieces = jnp.where(
        lane_piece == 0,
        high,
        jnp.where(lane_piece == 1, middle, jnp.where(lane_piece == 2, low, 0.0)),
    )
    xg[q, c, z, :, features:] = pieces.astype(jnp.bfloat16)
    pl.semaphore_wait(barrier, len(partners))

    sends = []

    def send(src, dst, send_sem, recv_sem, to):
        copy = pltpu.make_async_remote_copy(
            src_ref=src,
            dst_ref=dst,
            send_sem=send_sem,
            recv_sem=recv_sem,
            device_id=to,
            device_id_type=pl.DeviceIdType.MESH,
        )
        copy.start()
        sends.append(copy)

    def arrived(dst, recv_sem):
        pltpu.make_async_remote_copy(
            src_ref=dst,
            dst_ref=dst,
            send_sem=x_send_s.at[0, 0],
            recv_sem=recv_sem,
            device_id=sibling,
            device_id_type=pl.DeviceIdType.MESH,
        ).wait_recv()

    def send_rows(at, send_sem, to):
        send(xg.at[at], xg.at[at], send_sem, x_recv.at[at], to)

    def rows_arrived(at):
        arrived(xg.at[at], x_recv.at[at])

    def forward_a(k):
        at = (qa, c, near[k])
        rows_arrived(at)
        send_rows(at, x_send_b.at[1, k], along_b)
        send_rows(at, x_send_s.at[1, k], sibling)

    for k in range(nz - 1):
        send_rows((q, c, z), x_send_z.at[k], device(peers[k], q, c))
    send_rows((q, c, z), x_send_a.at[0], along_a)
    send_rows((q, c, z), x_send_b.at[0, 0], along_b)
    send_rows((q, c, z), x_send_s.at[0, 0], sibling)
    for k in range(1, nz):
        at = (q, c, near[k])
        rows_arrived(at)
        send_rows(at, x_send_a.at[k], along_a)
        send_rows(at, x_send_b.at[0, k], along_b)
        send_rows(at, x_send_s.at[0, k], sibling)
        forward_a(k - 1)
    forward_a(nz - 1)

    def experts_on(blocks):
        def gathered():
            return jnp.concatenate(
                [xg[bq, bc, :, :, :features].reshape(nz * rows, features) for bq, bc in blocks],
                axis=0,
            )

        tail = jnp.concatenate(
            [xg[bq, bc, :, :, features:].reshape(nz * rows, LANES) for bq, bc in blocks], axis=0
        ).astype(jnp.float32)
        tail_lane = lax.broadcasted_iota(jnp.int32, tail.shape, 1)
        scale = jnp.sum(
            jnp.where(lax.rem(tail_lane, experts) == expert, tail, 0.0), axis=1, keepdims=True
        )

        def hidden_tile(j, carry):
            columns = pl.ds(pl.multiple_of(j * FF_TILE, FF_TILE), FF_TILE)
            gate = jnp.dot(gathered(), gate_w[:, columns], preferred_element_type=jnp.float32)
            upper = jnp.dot(gathered(), up_w[:, columns], preferred_element_type=jnp.float32)
            silu = gate / (1.0 + jnp.exp(-gate))
            act[:, columns] = (scale * (silu * upper)).astype(jnp.bfloat16)
            return carry

        def out_tile(j, carry):
            columns = pl.ds(pl.multiple_of(j * OUT_TILE, OUT_TILE), OUT_TILE)
            result = jnp.dot(
                act[...], down_w[:, columns], preferred_element_type=jnp.float32
            ).astype(jnp.bfloat16)
            for number, (bq, bc) in enumerate(blocks):
                part[bq, bc, :, :, columns] = result[
                    number * nz * rows : (number + 1) * nz * rows
                ].reshape(nz, rows, OUT_TILE)
            return carry

        lax.fori_loop(0, hidden // FF_TILE, hidden_tile, 0)
        lax.fori_loop(0, features // OUT_TILE, out_tile, 0)

    def f32(ref, *at):
        return ref[at].astype(jnp.float32)

    def send_half(at):
        send(part.at[at, s], rs.at[at], rs_send.at[at], rs_recv.at[at], sibling)

    def half_arrived(at):
        arrived(rs.at[at], rs_recv.at[at])

    for k in range(nz):
        rows_arrived((q, s, near[k]))
        rows_arrived((qb, s, near[k]))
    for load in loads:
        load.wait()
    experts_on([(q, c), (q, s), (qa, c), (qb, s)])
    send_half(q)
    send_half(qb)
    for k in range(nz):
        for number, at in ((2, (qb, c, near[k])), (3, (qd, c, near[k]))):
            rows_arrived(at)
            send_rows(at, x_send_s.at[number, k], sibling)

    far = [near[k] for k in range(nz - 1, -1, -1)]
    half_arrived(q)
    half_arrived(qa)
    for k in range(nz):
        at = far[k]
        part[qa, c, at] = (f32(part, qa, c, at) + f32(rs, qa, at)).astype(jnp.bfloat16)
        send(part.at[qa, c, at], r1.at[0, at], r1_send.at[0, k], r1_recv.at[0, at], along_a)

    for k in range(nz):
        rows_arrived((qa, s, near[k]))
        rows_arrived((qd, s, near[k]))
    experts_on([(qd, c), (qd, s), (qb, c), (qa, s)])
    send_half(qd)
    send_half(qa)
    half_arrived(qd)
    for k in range(nz):
        at = far[k]
        part[qd, c, at] = (f32(part, qd, c, at) + f32(rs, qd, at)).astype(jnp.bfloat16)
        send(part.at[qd, c, at], r1.at[1, at], r1_send.at[1, k], r1_recv.at[1, at], along_a)
    half_arrived(qb)

    def sum_b(k):
        at = far[k]
        arrived(r1.at[1, at], r1_recv.at[1, at])
        part[qb, c, at] = (
            f32(part, qb, c, at) + f32(rs, qb, at) + f32(r1, 1, at)
        ).astype(jnp.bfloat16)
        send(part.at[qb, c, at], r2.at[at], r2_send.at[k], r2_recv.at[at], along_b)

    def sum_own(k):
        at = far[k]
        arrived(r1.at[0, at], r1_recv.at[0, at])
        arrived(r2.at[at], r2_recv.at[at])
        return f32(part, q, c, at) + f32(rs, q, at) + f32(r1, 0, at) + f32(r2, at)

    sum_b(0)
    for k in range(nz - 1):
        sum_b(k + 1)
        at = far[k]
        part[q, c, at] = sum_own(k).astype(jnp.bfloat16)
        send(part.at[q, c, at], rz.at[z], rz_send.at[k], rz_recv.at[z], device(at, q, c))
    total = sum_own(nz - 1)
    for peer in peers:
        arrived(rz.at[peer], rz_recv.at[peer])
        total += f32(rz, peer)
    out_ref[...] = total.reshape(steps, tok_rows, features).astype(out_ref.dtype)
    for copy in sends:
        copy.wait_send()


def fused(tokens, expert_ids, route_weight, gate_weight, up_weight, down_weight):
    device_count = lax.axis_size("ep")
    nz = device_count // (SQUARE * CORES)
    steps, tok_rows, features = tokens.shape
    hidden = gate_weight.shape[2]
    rows = steps * tok_rows
    group = nz * rows
    kind = tokens.dtype
    dma = pltpu.SemaphoreType.DMA
    vmem = pl.BlockSpec(memory_space=pltpu.VMEM)
    hbm = pl.BlockSpec(memory_space=pl.ANY)
    weight_bytes = 3 * features * hidden * 2
    return pl.pallas_call(
        functools.partial(fused_kernel, nz),
        out_shape=jax.ShapeDtypeStruct(tokens.shape, kind),
        in_specs=[vmem, vmem, vmem, hbm, hbm, hbm],
        out_specs=vmem,
        scratch_shapes=[
            pltpu.VMEM((features, hidden), kind),
            pltpu.VMEM((features, hidden), kind),
            pltpu.VMEM((hidden, features), kind),
            pltpu.VMEM((SQUARE, CORES, nz, rows, features + LANES), kind),
            pltpu.VMEM((SQUARE * group, hidden), kind),
            pltpu.VMEM((SQUARE, CORES, nz, rows, features), kind),
            pltpu.VMEM((SQUARE, nz, rows, features), kind),
            pltpu.VMEM((2, nz, rows, features), kind),
            pltpu.VMEM((nz, rows, features), kind),
            pltpu.VMEM((nz, rows, features), kind),
            dma((3,)),
            dma((SQUARE, CORES, nz)),
            dma((nz,)),
            dma((nz,)),
            dma((2, nz)),
            dma((SQUARE, nz)),
            dma((SQUARE,)),
            dma((SQUARE,)),
            dma((2, nz)),
            dma((2, nz)),
            dma((nz,)),
            dma((nz,)),
            dma((nz,)),
            dma((nz,)),
        ],
        compiler_params=pltpu.CompilerParams(
            collective_id=0, has_side_effects=True, vmem_limit_bytes=56 * 1024 * 1024
        ),
        cost_estimate=pl.CostEstimate(
            flops=2 * device_count * rows * 3 * features * hidden,
            bytes_accessed=weight_bytes,
            transcendentals=device_count * rows * hidden,
        ),
    )(tokens, expert_ids, route_weight, gate_weight, up_weight, down_weight)


def shards(tokens, expert_ids, route_weight, gate_weight, up_weight, down_weight):
    device_count = lax.axis_size("ep")
    expert_count = device_count // 2
    tok_rows = tokens.shape[1]
    features = tokens.shape[2]
    capacity = min(tok_rows, 2 * tok_rows * TOP // expert_count)
    every_row = capacity == tok_rows and device_count % (SQUARE * CORES) == 0
    if every_row and STEPS * tok_rows % 16 == 0:
        return fused(tokens, expert_ids, route_weight, gate_weight, up_weight, down_weight)
    half_slots = capacity // 2
    gate_m = gate_weight[0]
    up_m = up_weight[0]
    down_m = down_weight[0]
    parity_odd = lax.axis_index("ep") % 2 == 1
    layouts = []
    outgoing = []
    for step_index in range(STEPS):
        slot_index, slot_source = slot_layout(expert_ids[step_index], expert_count, capacity)
        padded = jnp.concatenate(
            [tokens[step_index], jnp.zeros((1, features), tokens.dtype)], axis=0
        )
        blocks = padded[slot_source // TOP].reshape(expert_count, capacity, features)
        arrange_paired = blocks.reshape(expert_count, half_slots, 2, features)
        arrange_paired = jnp.where(parity_odd, arrange_paired[:, :, ::-1], arrange_paired)
        outgoing.append(
            arrange_paired.transpose(0, 2, 1, 3).reshape(device_count, half_slots, features)
        )
        layouts.append(slot_index)
    returned_list = []
    for sent in outgoing:
        received = lax.all_to_all(sent, "ep", split_axis=0, concat_axis=0, tiled=True)
        partner = partner_2(received, "ep", 0)
        width = received.shape[1]
        apply_received = jnp.concatenate([received, partner], axis=1)
        gate = jnp.einsum("scd,df->scf", apply_received, gate_m, preferred_element_type=jnp.float32)
        upper = jnp.einsum("scd,df->scf", apply_received, up_m, preferred_element_type=jnp.float32)
        act = (jax.nn.silu(gate) * upper).astype(jnp.bfloat16)
        parts = jnp.einsum("scf,fd->scd", act, down_m, preferred_element_type=jnp.float32).astype(
            jnp.bfloat16
        )
        back = partner_2(parts[:, width:], "ep", 0)
        summed = (parts[:, :width].astype(jnp.float32) + back.astype(jnp.float32)).astype(
            jnp.bfloat16
        )
        returned_list.append(lax.all_to_all(summed, "ep", split_axis=0, concat_axis=0, tiled=True))
    answers = []
    for step_index in range(STEPS):
        returned = returned_list[step_index]
        paired = returned.reshape(expert_count, 2, half_slots, features).transpose(0, 2, 1, 3)
        paired = jnp.where(parity_odd, paired[:, :, ::-1], paired)
        answers.append(paired.reshape(expert_count, capacity, features))
    outputs = []
    for step_index in range(STEPS):
        flattened = answers[step_index].reshape(expert_count * capacity, features)
        picked = flattened[layouts[step_index]].reshape(tok_rows, TOP, features)
        summed = jnp.sum(route_weight[step_index][:, :, None] * picked.astype(jnp.float32), axis=1)
        outputs.append(summed.astype(jnp.bfloat16))
    return jnp.stack(outputs)


def solution(mesh):
    in_specs = (
        P(None, ("groups", "ep"), None),
        P(None, ("groups", "ep"), None),
        P(None, ("groups", "ep"), None),
        P("ep", None, None),
        P("ep", None, None),
        P("ep", None, None),
    )
    out_specs = P(None, ("groups", "ep"), None)
    return jax.shard_map(shards, mesh=mesh, in_specs=in_specs, out_specs=out_specs, check_vma=False)
```

```python
import functools

import jax
import jax.numpy as jnp
from jax import lax
from jax.experimental import pallas as pl
from jax.experimental.pallas import tpu as pltpu
from jax.sharding import PartitionSpec as P

TOP = 8
STEPS = 2


def partner_2(block, axis, apart):
    count = lax.axis_size(axis)
    route = []
    for low in range(count):
        high = low | 1 << apart
        if high != low and high < count:
            route += [(low, high), (high, low)]
    return lax.ppermute(block, axis, route)


def slot_layout(block_ids, expert_count, capacity):
    pairs = block_ids.reshape(-1)
    count = pairs.shape[0]
    one_hot = (pairs[:, None] == jnp.arange(expert_count, dtype=jnp.int32)[None, :]).astype(
        jnp.float32
    )
    order = jnp.arange(count, dtype=jnp.int32)
    earlier = (order[None, :] < order[:, None]).astype(jnp.float32)
    before = jnp.dot(earlier, one_hot, precision=lax.Precision.HIGHEST)
    slot_rank = jnp.sum(before * one_hot, axis=1).astype(jnp.int32)
    slot_index = pairs * capacity + slot_rank
    slot_source = jnp.full((expert_count * capacity,), count, jnp.int32).at[slot_index].set(order)
    return (slot_index, slot_source)


LANES = 128
SQUARE = 4
CORES = 2
FF_TILE = 256
OUT_TILE = 512


def peer_at(k, z, nz):
    low = lax.div(2 * (nz - 1 - z) + 1, nz)
    at = z * low + (nz - 1 - z) * (1 - low)
    other = k + lax.div(k - at + nz, nz)
    return other * low + (nz - 1 - other) * (1 - low)


OWN, FIRST, DIAGONAL, SECOND = 0, 2, 4, 6


def fused_kernel(
    nz, tok_ref, ids_ref, route_ref, gate_hbm, up_hbm, down_hbm, out_ref,
    gate_w, up_w, down_w, xg, act, part, rs, r1, r2, rz,
    w_sem, x_recv, x_send_z, x_send_a, x_send_b, x_send_s,
    rs_send, rs_recv, r1_send, r1_recv, r2_send, r2_recv, rz_send, rz_recv,
):
    steps, tok_rows, features = tok_ref.shape
    rows = steps * tok_rows
    hidden = act.shape[1]
    experts = nz * SQUARE
    me = lax.axis_index("ep")
    c = lax.rem(me, CORES)
    expert = lax.div(me, CORES)
    q = lax.rem(expert, SQUARE)
    z = lax.div(expert, SQUARE)
    x, y = lax.rem(q, 2), lax.div(q, 2)
    qx, qy = 2 * y + 1 - x, 2 * (1 - y) + x
    qa = qx * (1 - c) + qy * c
    qb = qy * (1 - c) + qx * c

    def device(to_z, to_q, to_c):
        return {"ep": (to_z * SQUARE + to_q) * CORES + to_c}

    sibling, along_a, along_b = device(z, q, 1 - c), device(z, qa, c), device(z, qb, c)
    peers = [peer_at(k, z, nz) for k in range(nz - 1)]
    near = [z] + peers
    far = near[::-1]

    loads = [
        pltpu.make_async_copy(gate_hbm.at[0], gate_w, w_sem.at[0]),
        pltpu.make_async_copy(up_hbm.at[0], up_w, w_sem.at[1]),
        pltpu.make_async_copy(down_hbm.at[0], down_w, w_sem.at[2]),
    ]
    barrier = pltpu.get_barrier_semaphore()
    partners = [device(p, q, c) for p in peers] + [along_a, along_b, sibling]
    for partner in partners:
        pl.semaphore_signal(
            barrier, inc=1, device_id=partner, device_id_type=pl.DeviceIdType.MESH
        )
    for load in loads:
        load.start()

    xg[OWN, z, :, :features] = (
        tok_ref[...].astype(jnp.float32).reshape(rows, features).astype(jnp.bfloat16)
    )
    lane = lax.broadcasted_iota(jnp.int32, (rows, LANES), 1)
    lane_expert, lane_piece = lax.rem(lane, experts), lax.div(lane, experts)
    ids = ids_ref[...].reshape(rows, TOP)
    route = route_ref[...].reshape(rows, TOP)
    coef = jnp.zeros((rows, LANES), jnp.float32)
    for k in range(TOP):
        coef += jnp.where(ids[:, k : k + 1] == lane_expert, route[:, k : k + 1], 0.0)
    high = coef.astype(jnp.bfloat16).astype(jnp.float32)
    middle = (coef - high).astype(jnp.bfloat16).astype(jnp.float32)
    low = coef - high - middle
    pieces = jnp.where(
        lane_piece == 0,
        high,
        jnp.where(lane_piece == 1, middle, jnp.where(lane_piece == 2, low, 0.0)),
    )
    xg[OWN, z, :, features:] = pieces.astype(jnp.bfloat16)
    pl.semaphore_wait(barrier, len(partners))

    sends = []

    def send(src, dst, send_sem, recv_sem, to):
        copy = pltpu.make_async_remote_copy(
            src_ref=src,
            dst_ref=dst,
            send_sem=send_sem,
            recv_sem=recv_sem,
            device_id=to,
            device_id_type=pl.DeviceIdType.MESH,
        )
        copy.start()
        sends.append(copy)

    def arrived(dst, recv_sem):
        pltpu.make_async_remote_copy(
            src_ref=dst,
            dst_ref=dst,
            send_sem=x_send_s.at[0, 0],
            recv_sem=recv_sem,
            device_id=sibling,
            device_id_type=pl.DeviceIdType.MESH,
        ).wait_recv()

    def send_rows(place, at, there, send_sem, to):
        send(xg.at[place, at], xg.at[there, at], send_sem, x_recv.at[there, at], to)

    def rows_arrived(place, at):
        arrived(xg.at[place, at], x_recv.at[place, at])

    def pass_own(k):
        send_rows(OWN, near[k], FIRST, x_send_a.at[k], along_a)
        send_rows(OWN, near[k], SECOND, x_send_b.at[0, k], along_b)
        send_rows(OWN, near[k], OWN + 1, x_send_s.at[0, k], sibling)

    def pass_first(k):
        rows_arrived(FIRST, near[k])
        send_rows(FIRST, near[k], DIAGONAL, x_send_b.at[1, k], along_b)
        send_rows(FIRST, near[k], FIRST + 1, x_send_s.at[1, k], sibling)

    def pass_last(place, k):
        rows_arrived(place, near[k])
        send_rows(place, near[k], place + 1, x_send_s.at[place // 2, k], sibling)

    for k in range(nz - 1):
        send_rows(OWN, z, OWN, x_send_z.at[k], device(peers[k], q, c))
    pass_own(0)
    late = []
    for k in range(1, nz):
        rows_arrived(OWN, near[k])
        pass_own(k)
        pass_first(k - 1)
        if k >= 2:
            pass_last(SECOND, k - 2)
    pass_first(nz - 1)
    if nz >= 2:
        pass_last(SECOND, nz - 2)
    for k in range(max(nz - 2, 0)):
        pass_last(DIAGONAL, k)
    late.append((SECOND, nz - 1))
    for k in range(max(nz - 2, 0), nz):
        late.append((DIAGONAL, k))

    tiles = features // OUT_TILE
    groups = [(0, (tiles + 1) // 2), ((tiles + 1) // 2, tiles)]
    group_columns = [pl.ds(lo * OUT_TILE, (hi - lo) * OUT_TILE) for lo, hi in groups]

    def experts_on(first, between):
        places = pl.ds(first, SQUARE)
        count = SQUARE * nz * rows
        tail = xg[places, :, :, features:].reshape(count, LANES).astype(jnp.float32)
        tail_lane = lax.broadcasted_iota(jnp.int32, tail.shape, 1)
        scale = jnp.sum(
            jnp.where(lax.rem(tail_lane, experts) == expert, tail, 0.0), axis=1, keepdims=True
        )
        for tile in range(hidden // FF_TILE):
            columns = pl.ds(tile * FF_TILE, FF_TILE)
            inputs = xg[places, :, :, :features].reshape(count, features)
            gate = jnp.dot(inputs, gate_w[:, columns], preferred_element_type=jnp.float32)
            upper = jnp.dot(inputs, up_w[:, columns], preferred_element_type=jnp.float32)
            silu = gate / (1.0 + jnp.exp(-gate))
            act[:, columns] = (scale * (silu * upper)).astype(jnp.bfloat16)
            if between:
                pass_last(*between.pop(0))
        for number, (lo, hi) in enumerate(groups):
            for tile in range(lo, hi):
                columns = pl.ds(tile * OUT_TILE, OUT_TILE)
                result = jnp.dot(
                    act[...], down_w[:, columns], preferred_element_type=jnp.float32
                ).astype(jnp.bfloat16)
                part[places, :, :, columns] = result.reshape(SQUARE, nz, rows, OUT_TILE)
                if between:
                    pass_last(*between.pop(0))
            columns = group_columns[number]
            for place in (first, first + 2):
                half = place // 2
                send(
                    part.at[place + 1, :, :, columns],
                    rs.at[half, :, :, columns],
                    rs_send.at[half, number],
                    rs_recv.at[half, number],
                    sibling,
                )
        while between:
            pass_last(*between.pop(0))

    def half_arrived(place):
        for number, columns in enumerate(group_columns):
            arrived(rs.at[place // 2, :, :, columns], rs_recv.at[place // 2, number])

    def f32(ref, *at):
        return ref[at].astype(jnp.float32)

    def both(place, at):
        return f32(part, place, at) + f32(rs, place // 2, at)

    def keep(place, at, value):
        part[place, at] = value.astype(jnp.bfloat16)

    for k in range(nz):
        rows_arrived(OWN + 1, near[k])
        rows_arrived(FIRST + 1, near[k])
    for load in loads:
        load.wait()
    experts_on(OWN, late)

    half_arrived(OWN)
    half_arrived(FIRST)
    for k in range(nz):
        at = far[k]
        keep(FIRST, at, both(FIRST, at))
        send(part.at[FIRST, at], r1.at[0, at], r1_send.at[0, k], r1_recv.at[0, at], along_a)

    for k in range(nz):
        rows_arrived(SECOND + 1, near[k])
        rows_arrived(DIAGONAL + 1, near[k])
    experts_on(DIAGONAL, [])
    half_arrived(DIAGONAL)
    for k in range(nz):
        at = far[k]
        keep(DIAGONAL, at, both(DIAGONAL, at))
        send(part.at[DIAGONAL, at], r1.at[1, at], r1_send.at[1, k], r1_recv.at[1, at], along_a)
    half_arrived(SECOND)

    def sum_second(k):
        at = far[k]
        arrived(r1.at[1, at], r1_recv.at[1, at])
        keep(SECOND, at, both(SECOND, at) + f32(r1, 1, at))
        send(part.at[SECOND, at], r2.at[at], r2_send.at[k], r2_recv.at[at], along_b)

    def sum_own(k):
        at = far[k]
        arrived(r1.at[0, at], r1_recv.at[0, at])
        arrived(r2.at[at], r2_recv.at[at])
        return both(OWN, at) + f32(r1, 0, at) + f32(r2, at)

    sum_second(0)
    for k in range(nz - 1):
        sum_second(k + 1)
        at = far[k]
        keep(OWN, at, sum_own(k))
        send(part.at[OWN, at], rz.at[z], rz_send.at[k], rz_recv.at[z], device(at, q, c))
    total = sum_own(nz - 1)
    for peer in peers:
        arrived(rz.at[peer], rz_recv.at[peer])
        total += f32(rz, peer)
    out_ref[...] = total.reshape(steps, tok_rows, features).astype(out_ref.dtype)
    for copy in sends:
        copy.wait_send()


def fused(tokens, expert_ids, route_weight, gate_weight, up_weight, down_weight):
    device_count = lax.axis_size("ep")
    nz = device_count // (SQUARE * CORES)
    steps, tok_rows, features = tokens.shape
    hidden = gate_weight.shape[2]
    rows = steps * tok_rows
    group = nz * rows
    kind = tokens.dtype
    dma = pltpu.SemaphoreType.DMA
    vmem = pl.BlockSpec(memory_space=pltpu.VMEM)
    hbm = pl.BlockSpec(memory_space=pl.ANY)
    weight_bytes = 3 * features * hidden * 2
    return pl.pallas_call(
        functools.partial(fused_kernel, nz),
        out_shape=jax.ShapeDtypeStruct(tokens.shape, kind),
        in_specs=[vmem, vmem, vmem, hbm, hbm, hbm],
        out_specs=vmem,
        scratch_shapes=[
            pltpu.VMEM((features, hidden), kind),
            pltpu.VMEM((features, hidden), kind),
            pltpu.VMEM((hidden, features), kind),
            pltpu.VMEM((SQUARE * CORES, nz, rows, features + LANES), kind),
            pltpu.VMEM((SQUARE * group, hidden), kind),
            pltpu.VMEM((SQUARE * CORES, nz, rows, features), kind),
            pltpu.VMEM((SQUARE, nz, rows, features), kind),
            pltpu.VMEM((2, nz, rows, features), kind),
            pltpu.VMEM((nz, rows, features), kind),
            pltpu.VMEM((nz, rows, features), kind),
            dma((3,)),
            dma((SQUARE * CORES, nz)),
            dma((nz,)),
            dma((nz,)),
            dma((2, nz)),
            dma((SQUARE, nz)),
            dma((SQUARE, 2)),
            dma((SQUARE, 2)),
            dma((2, nz)),
            dma((2, nz)),
            dma((nz,)),
            dma((nz,)),
            dma((nz,)),
            dma((nz,)),
        ],
        compiler_params=pltpu.CompilerParams(
            collective_id=0, has_side_effects=True, vmem_limit_bytes=56 * 1024 * 1024
        ),
        cost_estimate=pl.CostEstimate(
            flops=2 * device_count * rows * 3 * features * hidden,
            bytes_accessed=weight_bytes,
            transcendentals=device_count * rows * hidden,
        ),
    )(tokens, expert_ids, route_weight, gate_weight, up_weight, down_weight)


def shards(tokens, expert_ids, route_weight, gate_weight, up_weight, down_weight):
    device_count = lax.axis_size("ep")
    expert_count = device_count // 2
    tok_rows = tokens.shape[1]
    features = tokens.shape[2]
    capacity = min(tok_rows, 2 * tok_rows * TOP // expert_count)
    every_row = capacity == tok_rows and device_count % (SQUARE * CORES) == 0
    if every_row and STEPS * tok_rows % 16 == 0:
        return fused(tokens, expert_ids, route_weight, gate_weight, up_weight, down_weight)
    half_slots = capacity // 2
    gate_m = gate_weight[0]
    up_m = up_weight[0]
    down_m = down_weight[0]
    parity_odd = lax.axis_index("ep") % 2 == 1
    layouts = []
    outgoing = []
    for step_index in range(STEPS):
        slot_index, slot_source = slot_layout(expert_ids[step_index], expert_count, capacity)
        padded = jnp.concatenate(
            [tokens[step_index], jnp.zeros((1, features), tokens.dtype)], axis=0
        )
        blocks = padded[slot_source // TOP].reshape(expert_count, capacity, features)
        arrange_paired = blocks.reshape(expert_count, half_slots, 2, features)
        arrange_paired = jnp.where(parity_odd, arrange_paired[:, :, ::-1], arrange_paired)
        outgoing.append(
            arrange_paired.transpose(0, 2, 1, 3).reshape(device_count, half_slots, features)
        )
        layouts.append(slot_index)
    returned_list = []
    for sent in outgoing:
        received = lax.all_to_all(sent, "ep", split_axis=0, concat_axis=0, tiled=True)
        partner = partner_2(received, "ep", 0)
        width = received.shape[1]
        apply_received = jnp.concatenate([received, partner], axis=1)
        gate = jnp.einsum("scd,df->scf", apply_received, gate_m, preferred_element_type=jnp.float32)
        upper = jnp.einsum("scd,df->scf", apply_received, up_m, preferred_element_type=jnp.float32)
        act = (jax.nn.silu(gate) * upper).astype(jnp.bfloat16)
        parts = jnp.einsum("scf,fd->scd", act, down_m, preferred_element_type=jnp.float32).astype(
            jnp.bfloat16
        )
        back = partner_2(parts[:, width:], "ep", 0)
        summed = (parts[:, :width].astype(jnp.float32) + back.astype(jnp.float32)).astype(
            jnp.bfloat16
        )
        returned_list.append(lax.all_to_all(summed, "ep", split_axis=0, concat_axis=0, tiled=True))
    answers = []
    for step_index in range(STEPS):
        returned = returned_list[step_index]
        paired = returned.reshape(expert_count, 2, half_slots, features).transpose(0, 2, 1, 3)
        paired = jnp.where(parity_odd, paired[:, :, ::-1], paired)
        answers.append(paired.reshape(expert_count, capacity, features))
    outputs = []
    for step_index in range(STEPS):
        flattened = answers[step_index].reshape(expert_count * capacity, features)
        picked = flattened[layouts[step_index]].reshape(tok_rows, TOP, features)
        summed = jnp.sum(route_weight[step_index][:, :, None] * picked.astype(jnp.float32), axis=1)
        outputs.append(summed.astype(jnp.bfloat16))
    return jnp.stack(outputs)


def solution(mesh):
    in_specs = (
        P(None, ("groups", "ep"), None),
        P(None, ("groups", "ep"), None),
        P(None, ("groups", "ep"), None),
        P("ep", None, None),
        P("ep", None, None),
        P("ep", None, None),
    )
    out_specs = P(None, ("groups", "ep"), None)
    return jax.shard_map(shards, mesh=mesh, in_specs=in_specs, out_specs=out_specs, check_vma=False)
```

```python
import functools

import jax
import jax.numpy as jnp
from jax import lax
from jax.experimental import pallas as pl
from jax.experimental.pallas import tpu as pltpu
from jax.sharding import PartitionSpec as P

TOP = 8
STEPS = 2


def partner_2(block, axis, apart):
    count = lax.axis_size(axis)
    route = []
    for low in range(count):
        high = low | 1 << apart
        if high != low and high < count:
            route += [(low, high), (high, low)]
    return lax.ppermute(block, axis, route)


def slot_layout(block_ids, expert_count, capacity):
    pairs = block_ids.reshape(-1)
    count = pairs.shape[0]
    one_hot = (pairs[:, None] == jnp.arange(expert_count, dtype=jnp.int32)[None, :]).astype(
        jnp.float32
    )
    order = jnp.arange(count, dtype=jnp.int32)
    earlier = (order[None, :] < order[:, None]).astype(jnp.float32)
    before = jnp.dot(earlier, one_hot, precision=lax.Precision.HIGHEST)
    slot_rank = jnp.sum(before * one_hot, axis=1).astype(jnp.int32)
    slot_index = pairs * capacity + slot_rank
    slot_source = jnp.full((expert_count * capacity,), count, jnp.int32).at[slot_index].set(order)
    return (slot_index, slot_source)


LANES = 128
SQUARE = 4
CORES = 2
FF_TILE = 256
OUT_TILE = 512


def peer_at(k, z, nz):
    low = lax.div(2 * (nz - 1 - z) + 1, nz)
    at = z * low + (nz - 1 - z) * (1 - low)
    other = k + lax.div(k - at + nz, nz)
    return other * low + (nz - 1 - other) * (1 - low)


OWN, FIRST, DIAGONAL, SECOND = 0, 2, 4, 6


def fused_kernel(
    nz, tok_ref, ids_ref, route_ref, gate_hbm, up_hbm, down_hbm, out_ref,
    gate_w, up_w, down_w, xg, act, part, rs, r1, r2, rz,
    w_sem, x_recv, x_send_z, x_send_a, x_send_b, x_send_s,
    rs_send, rs_recv, r1_send, r1_recv, r2_send, r2_recv, rz_send, rz_recv,
):
    steps, tok_rows, features = tok_ref.shape
    rows = steps * tok_rows
    hidden = act.shape[1]
    experts = nz * SQUARE
    me = lax.axis_index("ep")
    c = lax.rem(me, CORES)
    expert = lax.div(me, CORES)
    q = lax.rem(expert, SQUARE)
    z = lax.div(expert, SQUARE)
    x, y = lax.rem(q, 2), lax.div(q, 2)
    qx, qy = 2 * y + 1 - x, 2 * (1 - y) + x
    qa = qx * (1 - c) + qy * c
    qb = qy * (1 - c) + qx * c

    def device(to_z, to_q, to_c):
        return {"ep": (to_z * SQUARE + to_q) * CORES + to_c}

    sibling, along_a, along_b = device(z, q, 1 - c), device(z, qa, c), device(z, qb, c)
    peers = [peer_at(k, z, nz) for k in range(nz - 1)]
    near = [z] + peers
    far = near[::-1]

    loads = [
        pltpu.make_async_copy(gate_hbm.at[0], gate_w, w_sem.at[0]),
        pltpu.make_async_copy(up_hbm.at[0], up_w, w_sem.at[1]),
        pltpu.make_async_copy(down_hbm.at[0], down_w, w_sem.at[2]),
    ]
    barrier = pltpu.get_barrier_semaphore()
    partners = [device(p, q, c) for p in peers] + [along_a, along_b, sibling]
    for partner in partners:
        pl.semaphore_signal(
            barrier, inc=1, device_id=partner, device_id_type=pl.DeviceIdType.MESH
        )
    for load in loads:
        load.start()

    xg[OWN, z, :, :features] = (
        tok_ref[...].astype(jnp.float32).reshape(rows, features).astype(jnp.bfloat16)
    )
    lane = lax.broadcasted_iota(jnp.int32, (rows, LANES), 1)
    lane_expert, lane_piece = lax.rem(lane, experts), lax.div(lane, experts)
    ids = ids_ref[...].reshape(rows, TOP)
    route = route_ref[...].reshape(rows, TOP)
    coef = jnp.zeros((rows, LANES), jnp.float32)
    for k in range(TOP):
        coef += jnp.where(ids[:, k : k + 1] == lane_expert, route[:, k : k + 1], 0.0)
    high = coef.astype(jnp.bfloat16).astype(jnp.float32)
    middle = (coef - high).astype(jnp.bfloat16).astype(jnp.float32)
    low = coef - high - middle
    pieces = jnp.where(
        lane_piece == 0,
        high,
        jnp.where(lane_piece == 1, middle, jnp.where(lane_piece == 2, low, 0.0)),
    )
    xg[OWN, z, :, features:] = pieces.astype(jnp.bfloat16)
    pl.semaphore_wait(barrier, len(partners))

    sends = []

    def send(src, dst, send_sem, recv_sem, to):
        copy = pltpu.make_async_remote_copy(
            src_ref=src,
            dst_ref=dst,
            send_sem=send_sem,
            recv_sem=recv_sem,
            device_id=to,
            device_id_type=pl.DeviceIdType.MESH,
        )
        copy.start()
        sends.append(copy)

    def arrived(dst, recv_sem):
        pltpu.make_async_remote_copy(
            src_ref=dst,
            dst_ref=dst,
            send_sem=x_send_s.at[0, 0],
            recv_sem=recv_sem,
            device_id=sibling,
            device_id_type=pl.DeviceIdType.MESH,
        ).wait_recv()

    def send_rows(place, at, there, send_sem, to):
        send(xg.at[place, at], xg.at[there, at], send_sem, x_recv.at[there, at], to)

    def rows_arrived(place, at):
        arrived(xg.at[place, at], x_recv.at[place, at])

    def pass_own(k):
        send_rows(OWN, near[k], FIRST, x_send_a.at[k], along_a)
        send_rows(OWN, near[k], SECOND, x_send_b.at[0, k], along_b)
        send_rows(OWN, near[k], OWN + 1, x_send_s.at[0, k], sibling)

    def pass_first(k):
        rows_arrived(FIRST, near[k])
        send_rows(FIRST, near[k], DIAGONAL, x_send_b.at[1, k], along_b)
        send_rows(FIRST, near[k], FIRST + 1, x_send_s.at[1, k], sibling)

    def pass_last(place, k):
        rows_arrived(place, near[k])
        send_rows(place, near[k], place + 1, x_send_s.at[place // 2, k], sibling)

    for k in range(nz - 1):
        send_rows(OWN, z, OWN, x_send_z.at[k], device(peers[k], q, c))
    pass_own(0)
    for k in range(1, nz):
        rows_arrived(OWN, near[k])
        pass_own(k)
        pass_first(k - 1)
        if k >= 2:
            pass_last(SECOND, k - 2)

    tiles = features // OUT_TILE
    groups = [(0, (tiles + 1) // 2), ((tiles + 1) // 2, tiles)]
    group_columns = [pl.ds(lo * OUT_TILE, (hi - lo) * OUT_TILE) for lo, hi in groups]

    def experts_on(first, between):
        between = list(between)

        def aside():
            if between:
                between.pop(0)()

        places = pl.ds(first, CORES)
        count = CORES * nz * rows
        tail = xg[places, :, :, features:].reshape(count, LANES).astype(jnp.float32)
        tail_lane = lax.broadcasted_iota(jnp.int32, tail.shape, 1)
        scale = jnp.sum(
            jnp.where(lax.rem(tail_lane, experts) == expert, tail, 0.0), axis=1, keepdims=True
        )
        for tile in range(hidden // FF_TILE):
            columns = pl.ds(tile * FF_TILE, FF_TILE)
            inputs = xg[places, :, :, :features].reshape(count, features)
            gate = jnp.dot(inputs, gate_w[:, columns], preferred_element_type=jnp.float32)
            upper = jnp.dot(inputs, up_w[:, columns], preferred_element_type=jnp.float32)
            silu = gate / (1.0 + jnp.exp(-gate))
            act[:, columns] = (scale * (silu * upper)).astype(jnp.bfloat16)
            aside()
        for number, (lo, hi) in enumerate(groups):
            for tile in range(lo, hi):
                columns = pl.ds(tile * OUT_TILE, OUT_TILE)
                result = jnp.dot(
                    act[...], down_w[:, columns], preferred_element_type=jnp.float32
                ).astype(jnp.bfloat16)
                part[places, :, :, columns] = result.reshape(CORES, nz, rows, OUT_TILE)
                aside()
            columns = group_columns[number]
            send(
                part.at[first + 1, :, :, columns],
                rs.at[first // 2, :, :, columns],
                rs_send.at[first // 2, number],
                rs_recv.at[first // 2, number],
                sibling,
            )
        while between:
            aside()

    def half_arrived(place):
        for number, columns in enumerate(group_columns):
            arrived(rs.at[place // 2, :, :, columns], rs_recv.at[place // 2, number])

    def f32(ref, *at):
        return ref[at].astype(jnp.float32)

    def both(place, at):
        return f32(part, place, at) + f32(rs, place // 2, at)

    def keep(place, at, value):
        part[place, at] = value.astype(jnp.bfloat16)

    def sibling_rows(place):
        for k in range(nz):
            rows_arrived(place + 1, near[k])

    def later(action, *at):
        return functools.partial(action, *at)

    def sum_first(k):
        at = far[k]
        if k == 0:
            half_arrived(FIRST)
        keep(FIRST, at, both(FIRST, at))
        send(part.at[FIRST, at], r1.at[0, at], r1_send.at[0, k], r1_recv.at[0, at], along_a)

    sibling_rows(OWN)
    for load in loads:
        load.wait()
    split = max(nz - 2, 0)
    asides = [later(pass_first, nz - 1)]
    asides += [later(pass_last, SECOND, k) for k in range(split, nz)]
    asides += [later(pass_last, DIAGONAL, k) for k in range(split)]
    experts_on(OWN, asides)
    sibling_rows(FIRST)
    experts_on(FIRST, [later(pass_last, DIAGONAL, k) for k in range(split, nz)])
    sibling_rows(SECOND)
    experts_on(SECOND, [lambda: None] + [later(sum_first, k) for k in range(nz)])
    sibling_rows(DIAGONAL)
    experts_on(DIAGONAL, [])
    half_arrived(OWN)
    half_arrived(DIAGONAL)
    for k in range(nz):
        at = far[k]
        keep(DIAGONAL, at, both(DIAGONAL, at))
        send(part.at[DIAGONAL, at], r1.at[1, at], r1_send.at[1, k], r1_recv.at[1, at], along_a)
    half_arrived(SECOND)

    def sum_second(k):
        at = far[k]
        arrived(r1.at[1, at], r1_recv.at[1, at])
        keep(SECOND, at, both(SECOND, at) + f32(r1, 1, at))
        send(part.at[SECOND, at], r2.at[at], r2_send.at[k], r2_recv.at[at], along_b)

    def sum_own(k):
        at = far[k]
        arrived(r1.at[0, at], r1_recv.at[0, at])
        arrived(r2.at[at], r2_recv.at[at])
        return both(OWN, at) + f32(r1, 0, at) + f32(r2, at)

    sum_second(0)
    for k in range(nz - 1):
        sum_second(k + 1)
        at = far[k]
        keep(OWN, at, sum_own(k))
        send(part.at[OWN, at], rz.at[z], rz_send.at[k], rz_recv.at[z], device(at, q, c))
    total = sum_own(nz - 1)
    for peer in peers:
        arrived(rz.at[peer], rz_recv.at[peer])
        total += f32(rz, peer)
    out_ref[...] = total.reshape(steps, tok_rows, features).astype(out_ref.dtype)
    for copy in sends:
        copy.wait_send()


def fused(tokens, expert_ids, route_weight, gate_weight, up_weight, down_weight):
    device_count = lax.axis_size("ep")
    nz = device_count // (SQUARE * CORES)
    steps, tok_rows, features = tokens.shape
    hidden = gate_weight.shape[2]
    rows = steps * tok_rows
    group = nz * rows
    kind = tokens.dtype
    dma = pltpu.SemaphoreType.DMA
    vmem = pl.BlockSpec(memory_space=pltpu.VMEM)
    hbm = pl.BlockSpec(memory_space=pl.ANY)
    weight_bytes = 3 * features * hidden * 2
    return pl.pallas_call(
        functools.partial(fused_kernel, nz),
        out_shape=jax.ShapeDtypeStruct(tokens.shape, kind),
        in_specs=[vmem, vmem, vmem, hbm, hbm, hbm],
        out_specs=vmem,
        scratch_shapes=[
            pltpu.VMEM((features, hidden), kind),
            pltpu.VMEM((features, hidden), kind),
            pltpu.VMEM((hidden, features), kind),
            pltpu.VMEM((SQUARE * CORES, nz, rows, features + LANES), kind),
            pltpu.VMEM((CORES * group, hidden), kind),
            pltpu.VMEM((SQUARE * CORES, nz, rows, features), kind),
            pltpu.VMEM((SQUARE, nz, rows, features), kind),
            pltpu.VMEM((2, nz, rows, features), kind),
            pltpu.VMEM((nz, rows, features), kind),
            pltpu.VMEM((nz, rows, features), kind),
            dma((3,)),
            dma((SQUARE * CORES, nz)),
            dma((nz,)),
            dma((nz,)),
            dma((2, nz)),
            dma((SQUARE, nz)),
            dma((SQUARE, 2)),
            dma((SQUARE, 2)),
            dma((2, nz)),
            dma((2, nz)),
            dma((nz,)),
            dma((nz,)),
            dma((nz,)),
            dma((nz,)),
        ],
        compiler_params=pltpu.CompilerParams(
            collective_id=0, has_side_effects=True, vmem_limit_bytes=56 * 1024 * 1024
        ),
        cost_estimate=pl.CostEstimate(
            flops=2 * device_count * rows * 3 * features * hidden,
            bytes_accessed=weight_bytes,
            transcendentals=device_count * rows * hidden,
        ),
    )(tokens, expert_ids, route_weight, gate_weight, up_weight, down_weight)


def shards(tokens, expert_ids, route_weight, gate_weight, up_weight, down_weight):
    device_count = lax.axis_size("ep")
    expert_count = device_count // 2
    tok_rows = tokens.shape[1]
    features = tokens.shape[2]
    capacity = min(tok_rows, 2 * tok_rows * TOP // expert_count)
    every_row = capacity == tok_rows and device_count % (SQUARE * CORES) == 0
    if every_row and STEPS * tok_rows % 16 == 0:
        return fused(tokens, expert_ids, route_weight, gate_weight, up_weight, down_weight)
    half_slots = capacity // 2
    gate_m = gate_weight[0]
    up_m = up_weight[0]
    down_m = down_weight[0]
    parity_odd = lax.axis_index("ep") % 2 == 1
    layouts = []
    outgoing = []
    for step_index in range(STEPS):
        slot_index, slot_source = slot_layout(expert_ids[step_index], expert_count, capacity)
        padded = jnp.concatenate(
            [tokens[step_index], jnp.zeros((1, features), tokens.dtype)], axis=0
        )
        blocks = padded[slot_source // TOP].reshape(expert_count, capacity, features)
        arrange_paired = blocks.reshape(expert_count, half_slots, 2, features)
        arrange_paired = jnp.where(parity_odd, arrange_paired[:, :, ::-1], arrange_paired)
        outgoing.append(
            arrange_paired.transpose(0, 2, 1, 3).reshape(device_count, half_slots, features)
        )
        layouts.append(slot_index)
    returned_list = []
    for sent in outgoing:
        received = lax.all_to_all(sent, "ep", split_axis=0, concat_axis=0, tiled=True)
        partner = partner_2(received, "ep", 0)
        width = received.shape[1]
        apply_received = jnp.concatenate([received, partner], axis=1)
        gate = jnp.einsum("scd,df->scf", apply_received, gate_m, preferred_element_type=jnp.float32)
        upper = jnp.einsum("scd,df->scf", apply_received, up_m, preferred_element_type=jnp.float32)
        act = (jax.nn.silu(gate) * upper).astype(jnp.bfloat16)
        parts = jnp.einsum("scf,fd->scd", act, down_m, preferred_element_type=jnp.float32).astype(
            jnp.bfloat16
        )
        back = partner_2(parts[:, width:], "ep", 0)
        summed = (parts[:, :width].astype(jnp.float32) + back.astype(jnp.float32)).astype(
            jnp.bfloat16
        )
        returned_list.append(lax.all_to_all(summed, "ep", split_axis=0, concat_axis=0, tiled=True))
    answers = []
    for step_index in range(STEPS):
        returned = returned_list[step_index]
        paired = returned.reshape(expert_count, 2, half_slots, features).transpose(0, 2, 1, 3)
        paired = jnp.where(parity_odd, paired[:, :, ::-1], paired)
        answers.append(paired.reshape(expert_count, capacity, features))
    outputs = []
    for step_index in range(STEPS):
        flattened = answers[step_index].reshape(expert_count * capacity, features)
        picked = flattened[layouts[step_index]].reshape(tok_rows, TOP, features)
        summed = jnp.sum(route_weight[step_index][:, :, None] * picked.astype(jnp.float32), axis=1)
        outputs.append(summed.astype(jnp.bfloat16))
    return jnp.stack(outputs)


def solution(mesh):
    in_specs = (
        P(None, ("groups", "ep"), None),
        P(None, ("groups", "ep"), None),
        P(None, ("groups", "ep"), None),
        P("ep", None, None),
        P("ep", None, None),
        P("ep", None, None),
    )
    out_specs = P(None, ("groups", "ep"), None)
    return jax.shard_map(shards, mesh=mesh, in_specs=in_specs, out_specs=out_specs, check_vma=False)
```

```python
import functools

import jax
import jax.numpy as jnp
from jax import lax
from jax.experimental import pallas as pl
from jax.experimental.pallas import tpu as pltpu
from jax.sharding import PartitionSpec as P

TOP = 8
STEPS = 2


def partner_2(block, axis, apart):
    count = lax.axis_size(axis)
    route = []
    for low in range(count):
        high = low | 1 << apart
        if high != low and high < count:
            route += [(low, high), (high, low)]
    return lax.ppermute(block, axis, route)


def slot_layout(block_ids, expert_count, capacity):
    pairs = block_ids.reshape(-1)
    count = pairs.shape[0]
    one_hot = (pairs[:, None] == jnp.arange(expert_count, dtype=jnp.int32)[None, :]).astype(
        jnp.float32
    )
    order = jnp.arange(count, dtype=jnp.int32)
    earlier = (order[None, :] < order[:, None]).astype(jnp.float32)
    before = jnp.dot(earlier, one_hot, precision=lax.Precision.HIGHEST)
    slot_rank = jnp.sum(before * one_hot, axis=1).astype(jnp.int32)
    slot_index = pairs * capacity + slot_rank
    slot_source = jnp.full((expert_count * capacity,), count, jnp.int32).at[slot_index].set(order)
    return (slot_index, slot_source)


LANES = 128
SQUARE = 4
CORES = 2
FF_TILE = 256
OUT_TILE = 512


OWN, FIRST, DIAGONAL, SECOND = 0, 2, 4, 6


def fused_kernel(
    nz, tok_ref, ids_ref, route_ref, gate_hbm, up_hbm, down_hbm, out_ref,
    gate_w, up_w, down_w, xg, act, part, rs, r1, r2, rz,
    w_sem, x_recv, x_send_z, x_send_a, x_send_b, x_send_s,
    rs_send, rs_recv, r1_send, r1_recv, r2_send, r2_recv, rz_send, rz_recv,
):
    steps, tok_rows, features = tok_ref.shape
    rows = steps * tok_rows
    hidden = act.shape[1]
    experts = nz * SQUARE
    me = lax.axis_index("ep")
    c = lax.rem(me, CORES)
    expert = lax.div(me, CORES)
    q = lax.rem(expert, SQUARE)
    z = lax.div(expert, SQUARE)
    x, y = lax.rem(q, 2), lax.div(q, 2)
    qx, qy = 2 * y + 1 - x, 2 * (1 - y) + x
    qa = qx * (1 - c) + qy * c
    qb = qy * (1 - c) + qx * c

    def device(to_z, to_q, to_c):
        return {"ep": (to_z * SQUARE + to_q) * CORES + to_c}

    sibling, along_a, along_b = device(z, q, 1 - c), device(z, qa, c), device(z, qb, c)
    mate = z + 1 - 2 * lax.rem(z, 2)
    across = [lax.rem(z + 2 * h, nz) for h in range(1, nz // 2)]
    near = [z, mate]
    for there in across:
        near += [there, there + mate - z]
    far = near[::-1]

    loads = [
        pltpu.make_async_copy(gate_hbm.at[0], gate_w, w_sem.at[0]),
        pltpu.make_async_copy(up_hbm.at[0], up_w, w_sem.at[1]),
        pltpu.make_async_copy(down_hbm.at[0], down_w, w_sem.at[2]),
    ]
    barrier = pltpu.get_barrier_semaphore()
    partners = [device(p, q, c) for p in [mate] + across] + [along_a, along_b, sibling]
    for partner in partners:
        pl.semaphore_signal(
            barrier, inc=1, device_id=partner, device_id_type=pl.DeviceIdType.MESH
        )
    for load in loads:
        load.start()

    xg[OWN, z, :, :features] = (
        tok_ref[...].astype(jnp.float32).reshape(rows, features).astype(jnp.bfloat16)
    )
    lane = lax.broadcasted_iota(jnp.int32, (rows, LANES), 1)
    lane_expert, lane_piece = lax.rem(lane, experts), lax.div(lane, experts)
    ids = ids_ref[...].reshape(rows, TOP)
    route = route_ref[...].reshape(rows, TOP)
    coef = jnp.zeros((rows, LANES), jnp.float32)
    for k in range(TOP):
        coef += jnp.where(ids[:, k : k + 1] == lane_expert, route[:, k : k + 1], 0.0)
    high = coef.astype(jnp.bfloat16).astype(jnp.float32)
    middle = (coef - high).astype(jnp.bfloat16).astype(jnp.float32)
    low = coef - high - middle
    pieces = jnp.where(
        lane_piece == 0,
        high,
        jnp.where(lane_piece == 1, middle, jnp.where(lane_piece == 2, low, 0.0)),
    )
    xg[OWN, z, :, features:] = pieces.astype(jnp.bfloat16)
    pl.semaphore_wait(barrier, len(partners))

    sends = []

    def send(src, dst, send_sem, recv_sem, to):
        copy = pltpu.make_async_remote_copy(
            src_ref=src,
            dst_ref=dst,
            send_sem=send_sem,
            recv_sem=recv_sem,
            device_id=to,
            device_id_type=pl.DeviceIdType.MESH,
        )
        copy.start()
        sends.append(copy)

    def arrived(dst, recv_sem):
        pltpu.make_async_remote_copy(
            src_ref=dst,
            dst_ref=dst,
            send_sem=x_send_s.at[0, 0],
            recv_sem=recv_sem,
            device_id=sibling,
            device_id_type=pl.DeviceIdType.MESH,
        ).wait_recv()

    def send_rows(place, at, there, send_sem, to):
        send(xg.at[place, at], xg.at[there, at], send_sem, x_recv.at[there, at], to)

    def rows_arrived(place, at):
        arrived(xg.at[place, at], x_recv.at[place, at])

    def pass_own(k):
        send_rows(OWN, near[k], FIRST, x_send_a.at[k], along_a)
        send_rows(OWN, near[k], SECOND, x_send_b.at[0, k], along_b)
        send_rows(OWN, near[k], OWN + 1, x_send_s.at[0, k], sibling)

    def pass_first(k):
        rows_arrived(FIRST, near[k])
        send_rows(FIRST, near[k], DIAGONAL, x_send_b.at[1, k], along_b)
        send_rows(FIRST, near[k], FIRST + 1, x_send_s.at[1, k], sibling)

    def pass_last(place, k):
        rows_arrived(place, near[k])
        send_rows(place, near[k], place + 1, x_send_s.at[place // 2, k], sibling)

    for number, there in enumerate(across):
        send_rows(OWN, z, OWN, x_send_z.at[2 * number], device(there, q, c))
    send_rows(OWN, z, OWN, x_send_z.at[nz - 1], device(mate, q, c))
    pass_own(0)
    for k in range(1, nz):
        rows_arrived(OWN, near[k])
        if k % 2 == 0:
            send_rows(OWN, near[k], OWN, x_send_z.at[k - 1], device(mate, q, c))
        pass_own(k)
        pass_first(k - 1)
        if k >= 2:
            pass_last(SECOND, k - 2)

    tiles = features // OUT_TILE
    groups = [(0, (tiles + 1) // 2), ((tiles + 1) // 2, tiles)]
    group_columns = [pl.ds(lo * OUT_TILE, (hi - lo) * OUT_TILE) for lo, hi in groups]

    def experts_on(first, between):
        between = list(between)

        def aside():
            if between:
                between.pop(0)()

        places = pl.ds(first, CORES)
        count = CORES * nz * rows
        tail = xg[places, :, :, features:].reshape(count, LANES).astype(jnp.float32)
        tail_lane = lax.broadcasted_iota(jnp.int32, tail.shape, 1)
        scale = jnp.sum(
            jnp.where(lax.rem(tail_lane, experts) == expert, tail, 0.0), axis=1, keepdims=True
        )
        for tile in range(hidden // FF_TILE):
            columns = pl.ds(tile * FF_TILE, FF_TILE)
            inputs = xg[places, :, :, :features].reshape(count, features)
            gate = jnp.dot(inputs, gate_w[:, columns], preferred_element_type=jnp.float32)
            upper = jnp.dot(inputs, up_w[:, columns], preferred_element_type=jnp.float32)
            silu = gate / (1.0 + jnp.exp(-gate))
            act[:, columns] = (scale * (silu * upper)).astype(jnp.bfloat16)
            aside()
        for number, (lo, hi) in enumerate(groups):
            for tile in range(lo, hi):
                columns = pl.ds(tile * OUT_TILE, OUT_TILE)
                result = jnp.dot(
                    act[...], down_w[:, columns], preferred_element_type=jnp.float32
                ).astype(jnp.bfloat16)
                part[places, :, :, columns] = result.reshape(CORES, nz, rows, OUT_TILE)
                aside()
            columns = group_columns[number]
            send(
                part.at[first + 1, :, :, columns],
                rs.at[first // 2, :, :, columns],
                rs_send.at[first // 2, number],
                rs_recv.at[first // 2, number],
                sibling,
            )
        while between:
            aside()

    def half_arrived(place):
        for number, columns in enumerate(group_columns):
            arrived(rs.at[place // 2, :, :, columns], rs_recv.at[place // 2, number])

    def f32(ref, *at):
        return ref[at].astype(jnp.float32)

    def both(place, at):
        return f32(part, place, at) + f32(rs, place // 2, at)

    def keep(place, at, value):
        part[place, at] = value.astype(jnp.bfloat16)

    def sibling_rows(place):
        for k in range(nz):
            rows_arrived(place + 1, near[k])

    def later(action, *at):
        return functools.partial(action, *at)

    def sum_first(k):
        at = far[k]
        if k == 0:
            half_arrived(FIRST)
        keep(FIRST, at, both(FIRST, at))
        send(part.at[FIRST, at], r1.at[0, at], r1_send.at[0, k], r1_recv.at[0, at], along_a)

    sibling_rows(OWN)
    for load in loads:
        load.wait()
    split = max(nz - 2, 0)
    asides = [later(pass_first, nz - 1)]
    asides += [later(pass_last, SECOND, k) for k in range(split, nz)]
    asides += [later(pass_last, DIAGONAL, k) for k in range(split)]
    experts_on(OWN, asides)
    sibling_rows(FIRST)
    experts_on(FIRST, [later(pass_last, DIAGONAL, k) for k in range(split, nz)])
    sibling_rows(SECOND)
    experts_on(SECOND, [lambda: None] + [later(sum_first, k) for k in range(nz)])
    sibling_rows(DIAGONAL)
    experts_on(DIAGONAL, [])
    half_arrived(OWN)
    half_arrived(DIAGONAL)
    for k in range(nz):
        at = far[k]
        keep(DIAGONAL, at, both(DIAGONAL, at))
        send(part.at[DIAGONAL, at], r1.at[1, at], r1_send.at[1, k], r1_recv.at[1, at], along_a)
    half_arrived(SECOND)

    def sum_second(k):
        at = far[k]
        arrived(r1.at[1, at], r1_recv.at[1, at])
        keep(SECOND, at, both(SECOND, at) + f32(r1, 1, at))
        send(part.at[SECOND, at], r2.at[at], r2_send.at[k], r2_recv.at[at], along_b)

    def sum_own(k):
        at = far[k]
        arrived(r1.at[0, at], r1_recv.at[0, at])
        arrived(r2.at[at], r2_recv.at[at])
        return both(OWN, at) + f32(r1, 0, at) + f32(r2, at)

    sum_second(0)
    for k in range(nz - 1):
        sum_second(k + 1)
        at = far[k]
        value = sum_own(k)
        if k % 2 == 0:
            keep(OWN, at, value)
            send(part.at[OWN, at], rz.at[k], rz_send.at[k], rz_recv.at[k], device(mate, q, c))
        else:
            arrived(rz.at[k - 1], rz_recv.at[k - 1])
            keep(OWN, at, value + f32(rz, k - 1))
            send(part.at[OWN, at], rz.at[k], rz_send.at[k], rz_recv.at[k], device(at, q, c))
    total = sum_own(nz - 1)
    for k in list(range(1, nz - 1, 2)) + [nz - 2]:
        arrived(rz.at[k], rz_recv.at[k])
        total += f32(rz, k)
    out_ref[...] = total.reshape(steps, tok_rows, features).astype(out_ref.dtype)
    for copy in sends:
        copy.wait_send()


def fused(tokens, expert_ids, route_weight, gate_weight, up_weight, down_weight):
    device_count = lax.axis_size("ep")
    nz = device_count // (SQUARE * CORES)
    steps, tok_rows, features = tokens.shape
    hidden = gate_weight.shape[2]
    rows = steps * tok_rows
    group = nz * rows
    kind = tokens.dtype
    dma = pltpu.SemaphoreType.DMA
    vmem = pl.BlockSpec(memory_space=pltpu.VMEM)
    hbm = pl.BlockSpec(memory_space=pl.ANY)
    weight_bytes = 3 * features * hidden * 2
    return pl.pallas_call(
        functools.partial(fused_kernel, nz),
        out_shape=jax.ShapeDtypeStruct(tokens.shape, kind),
        in_specs=[vmem, vmem, vmem, hbm, hbm, hbm],
        out_specs=vmem,
        scratch_shapes=[
            pltpu.VMEM((features, hidden), kind),
            pltpu.VMEM((features, hidden), kind),
            pltpu.VMEM((hidden, features), kind),
            pltpu.VMEM((SQUARE * CORES, nz, rows, features + LANES), kind),
            pltpu.VMEM((CORES * group, hidden), kind),
            pltpu.VMEM((SQUARE * CORES, nz, rows, features), kind),
            pltpu.VMEM((SQUARE, nz, rows, features), kind),
            pltpu.VMEM((2, nz, rows, features), kind),
            pltpu.VMEM((nz, rows, features), kind),
            pltpu.VMEM((nz, rows, features), kind),
            dma((3,)),
            dma((SQUARE * CORES, nz)),
            dma((nz,)),
            dma((nz,)),
            dma((2, nz)),
            dma((SQUARE, nz)),
            dma((SQUARE, 2)),
            dma((SQUARE, 2)),
            dma((2, nz)),
            dma((2, nz)),
            dma((nz,)),
            dma((nz,)),
            dma((nz,)),
            dma((nz,)),
        ],
        compiler_params=pltpu.CompilerParams(
            collective_id=0, has_side_effects=True, vmem_limit_bytes=56 * 1024 * 1024
        ),
        cost_estimate=pl.CostEstimate(
            flops=2 * device_count * rows * 3 * features * hidden,
            bytes_accessed=weight_bytes,
            transcendentals=device_count * rows * hidden,
        ),
    )(tokens, expert_ids, route_weight, gate_weight, up_weight, down_weight)


def shards(tokens, expert_ids, route_weight, gate_weight, up_weight, down_weight):
    device_count = lax.axis_size("ep")
    expert_count = device_count // 2
    tok_rows = tokens.shape[1]
    features = tokens.shape[2]
    capacity = min(tok_rows, 2 * tok_rows * TOP // expert_count)
    every_row = capacity == tok_rows and device_count % (2 * SQUARE * CORES) == 0
    if every_row and STEPS * tok_rows % 16 == 0:
        return fused(tokens, expert_ids, route_weight, gate_weight, up_weight, down_weight)
    half_slots = capacity // 2
    gate_m = gate_weight[0]
    up_m = up_weight[0]
    down_m = down_weight[0]
    parity_odd = lax.axis_index("ep") % 2 == 1
    layouts = []
    outgoing = []
    for step_index in range(STEPS):
        slot_index, slot_source = slot_layout(expert_ids[step_index], expert_count, capacity)
        padded = jnp.concatenate(
            [tokens[step_index], jnp.zeros((1, features), tokens.dtype)], axis=0
        )
        blocks = padded[slot_source // TOP].reshape(expert_count, capacity, features)
        arrange_paired = blocks.reshape(expert_count, half_slots, 2, features)
        arrange_paired = jnp.where(parity_odd, arrange_paired[:, :, ::-1], arrange_paired)
        outgoing.append(
            arrange_paired.transpose(0, 2, 1, 3).reshape(device_count, half_slots, features)
        )
        layouts.append(slot_index)
    returned_list = []
    for sent in outgoing:
        received = lax.all_to_all(sent, "ep", split_axis=0, concat_axis=0, tiled=True)
        partner = partner_2(received, "ep", 0)
        width = received.shape[1]
        apply_received = jnp.concatenate([received, partner], axis=1)
        gate = jnp.einsum("scd,df->scf", apply_received, gate_m, preferred_element_type=jnp.float32)
        upper = jnp.einsum("scd,df->scf", apply_received, up_m, preferred_element_type=jnp.float32)
        act = (jax.nn.silu(gate) * upper).astype(jnp.bfloat16)
        parts = jnp.einsum("scf,fd->scd", act, down_m, preferred_element_type=jnp.float32).astype(
            jnp.bfloat16
        )
        back = partner_2(parts[:, width:], "ep", 0)
        summed = (parts[:, :width].astype(jnp.float32) + back.astype(jnp.float32)).astype(
            jnp.bfloat16
        )
        returned_list.append(lax.all_to_all(summed, "ep", split_axis=0, concat_axis=0, tiled=True))
    answers = []
    for step_index in range(STEPS):
        returned = returned_list[step_index]
        paired = returned.reshape(expert_count, 2, half_slots, features).transpose(0, 2, 1, 3)
        paired = jnp.where(parity_odd, paired[:, :, ::-1], paired)
        answers.append(paired.reshape(expert_count, capacity, features))
    outputs = []
    for step_index in range(STEPS):
        flattened = answers[step_index].reshape(expert_count * capacity, features)
        picked = flattened[layouts[step_index]].reshape(tok_rows, TOP, features)
        summed = jnp.sum(route_weight[step_index][:, :, None] * picked.astype(jnp.float32), axis=1)
        outputs.append(summed.astype(jnp.bfloat16))
    return jnp.stack(outputs)


def solution(mesh):
    in_specs = (
        P(None, ("groups", "ep"), None),
        P(None, ("groups", "ep"), None),
        P(None, ("groups", "ep"), None),
        P("ep", None, None),
        P("ep", None, None),
        P("ep", None, None),
    )
    out_specs = P(None, ("groups", "ep"), None)
    return jax.shard_map(shards, mesh=mesh, in_specs=in_specs, out_specs=out_specs, check_vma=False)
```

```python
import functools

import jax
import jax.numpy as jnp
from jax import lax
from jax.experimental import pallas as pl
from jax.experimental.pallas import tpu as pltpu
from jax.sharding import PartitionSpec as P

TOP = 8
STEPS = 2


def partner_2(block, axis, apart):
    count = lax.axis_size(axis)
    route = []
    for low in range(count):
        high = low | 1 << apart
        if high != low and high < count:
            route += [(low, high), (high, low)]
    return lax.ppermute(block, axis, route)


def slot_layout(block_ids, expert_count, capacity):
    pairs = block_ids.reshape(-1)
    count = pairs.shape[0]
    one_hot = (pairs[:, None] == jnp.arange(expert_count, dtype=jnp.int32)[None, :]).astype(
        jnp.float32
    )
    order = jnp.arange(count, dtype=jnp.int32)
    earlier = (order[None, :] < order[:, None]).astype(jnp.float32)
    before = jnp.dot(earlier, one_hot, precision=lax.Precision.HIGHEST)
    slot_rank = jnp.sum(before * one_hot, axis=1).astype(jnp.int32)
    slot_index = pairs * capacity + slot_rank
    slot_source = jnp.full((expert_count * capacity,), count, jnp.int32).at[slot_index].set(order)
    return (slot_index, slot_source)


LANES = 128
SQUARE = 4
CORES = 2
FF_TILE = 256
OUT_TILE = 512


OWN, FIRST, DIAGONAL, SECOND = 0, 2, 4, 6


def fused_kernel(
    nz, tok_hbm, ids_hbm, route_hbm, gate_hbm, up_hbm, down_hbm, out_ref,
    tok_ref, ids_ref, route_ref, gate_w, up_w, down_w, xg, act, part, rs, r1, r2, rz,
    w_sem, x_recv, x_send_z, x_send_a, x_send_b, x_send_s,
    rs_send, rs_recv, r1_send, r1_recv, r2_send, r2_recv, rz_send, rz_recv,
):
    steps, tok_rows, features = tok_ref.shape
    rows = steps * tok_rows
    hidden = act.shape[1]
    experts = nz * SQUARE
    me = lax.axis_index("ep")
    c = lax.rem(me, CORES)
    expert = lax.div(me, CORES)
    q = lax.rem(expert, SQUARE)
    z = lax.div(expert, SQUARE)
    x, y = lax.rem(q, 2), lax.div(q, 2)
    qx, qy = 2 * y + 1 - x, 2 * (1 - y) + x
    qa = qx * (1 - c) + qy * c
    qb = qy * (1 - c) + qx * c

    def device(to_z, to_q, to_c):
        return {"ep": (to_z * SQUARE + to_q) * CORES + to_c}

    sibling, along_a, along_b = device(z, q, 1 - c), device(z, qa, c), device(z, qb, c)
    mate = z + 1 - 2 * lax.rem(z, 2)
    across = [lax.rem(z + 2 * h, nz) for h in range(1, nz // 2)]
    near = [z, mate]
    for there in across:
        near += [there, there + mate - z]
    crossings = len(across)
    far = near[3::2] + [mate] + across + [z]

    loads = [
        pltpu.make_async_copy(gate_hbm.at[0], gate_w, w_sem.at[0]),
        pltpu.make_async_copy(up_hbm.at[0], up_w, w_sem.at[1]),
        pltpu.make_async_copy(down_hbm.at[0], down_w, w_sem.at[2]),
    ]
    fetches = [
        pltpu.make_async_copy(tok_hbm, tok_ref, w_sem.at[3]),
        pltpu.make_async_copy(ids_hbm, ids_ref, w_sem.at[4]),
        pltpu.make_async_copy(route_hbm, route_ref, w_sem.at[5]),
    ]
    barrier = pltpu.get_barrier_semaphore()
    partners = [device(p, q, c) for p in [mate] + across] + [along_a, along_b, sibling]
    for partner in partners:
        pl.semaphore_signal(
            barrier, inc=1, device_id=partner, device_id_type=pl.DeviceIdType.MESH
        )
    for load in fetches + loads:
        load.start()
    for load in fetches:
        load.wait()

    xg[OWN, z, :, :features] = (
        tok_ref[...].astype(jnp.float32).reshape(rows, features).astype(jnp.bfloat16)
    )
    lane = lax.broadcasted_iota(jnp.int32, (rows, LANES), 1)
    lane_expert, lane_piece = lax.rem(lane, experts), lax.div(lane, experts)
    ids = ids_ref[...].reshape(rows, TOP)
    route = route_ref[...].reshape(rows, TOP)
    coef = jnp.zeros((rows, LANES), jnp.float32)
    for k in range(TOP):
        coef += jnp.where(ids[:, k : k + 1] == lane_expert, route[:, k : k + 1], 0.0)
    high = coef.astype(jnp.bfloat16).astype(jnp.float32)
    middle = (coef - high).astype(jnp.bfloat16).astype(jnp.float32)
    low = coef - high - middle
    pieces = jnp.where(
        lane_piece == 0,
        high,
        jnp.where(lane_piece == 1, middle, jnp.where(lane_piece == 2, low, 0.0)),
    )
    xg[OWN, z, :, features:] = pieces.astype(jnp.bfloat16)
    pl.semaphore_wait(barrier, len(partners))

    sends = []

    def send(src, dst, send_sem, recv_sem, to):
        copy = pltpu.make_async_remote_copy(
            src_ref=src,
            dst_ref=dst,
            send_sem=send_sem,
            recv_sem=recv_sem,
            device_id=to,
            device_id_type=pl.DeviceIdType.MESH,
        )
        copy.start()
        sends.append(copy)

    def arrived(dst, recv_sem):
        pltpu.make_async_remote_copy(
            src_ref=dst,
            dst_ref=dst,
            send_sem=x_send_s.at[0, 0],
            recv_sem=recv_sem,
            device_id=sibling,
            device_id_type=pl.DeviceIdType.MESH,
        ).wait_recv()

    def send_rows(place, at, there, send_sem, to):
        send(xg.at[place, at], xg.at[there, at], send_sem, x_recv.at[there, at], to)

    def rows_arrived(place, at):
        arrived(xg.at[place, at], x_recv.at[place, at])

    def pass_own(k):
        send_rows(OWN, near[k], FIRST, x_send_a.at[k], along_a)
        send_rows(OWN, near[k], SECOND, x_send_b.at[0, k], along_b)
        send_rows(OWN, near[k], OWN + 1, x_send_s.at[0, k], sibling)

    def pass_first(k):
        rows_arrived(FIRST, near[k])
        send_rows(FIRST, near[k], DIAGONAL, x_send_b.at[1, k], along_b)
        send_rows(FIRST, near[k], FIRST + 1, x_send_s.at[1, k], sibling)

    def pass_last(place, k):
        rows_arrived(place, near[k])
        send_rows(place, near[k], place + 1, x_send_s.at[place // 2, k], sibling)

    for number, there in enumerate(across):
        send_rows(OWN, z, OWN, x_send_z.at[2 * number], device(there, q, c))
    send_rows(OWN, z, OWN, x_send_z.at[nz - 1], device(mate, q, c))
    pass_own(0)
    for k in range(1, nz):
        rows_arrived(OWN, near[k])
        if k % 2 == 0:
            send_rows(OWN, near[k], OWN, x_send_z.at[k - 1], device(mate, q, c))
        pass_own(k)
        pass_first(k - 1)
        if k >= 2:
            pass_last(SECOND, k - 2)

    tiles = features // OUT_TILE
    groups = [(0, (tiles + 1) // 2), ((tiles + 1) // 2, tiles)]
    group_columns = [pl.ds(lo * OUT_TILE, (hi - lo) * OUT_TILE) for lo, hi in groups]

    def experts_on(first, between):
        between = list(between)

        def aside():
            if between:
                between.pop(0)()

        places = pl.ds(first, CORES)
        count = CORES * nz * rows
        tail = xg[places, :, :, features:].reshape(count, LANES).astype(jnp.float32)
        tail_lane = lax.broadcasted_iota(jnp.int32, tail.shape, 1)
        scale = jnp.sum(
            jnp.where(lax.rem(tail_lane, experts) == expert, tail, 0.0), axis=1, keepdims=True
        )
        for tile in range(hidden // FF_TILE):
            columns = pl.ds(tile * FF_TILE, FF_TILE)
            inputs = xg[places, :, :, :features].reshape(count, features)
            gate = jnp.dot(inputs, gate_w[:, columns], preferred_element_type=jnp.float32)
            upper = jnp.dot(inputs, up_w[:, columns], preferred_element_type=jnp.float32)
            silu = gate / (1.0 + jnp.exp(-gate))
            act[:, columns] = (scale * (silu * upper)).astype(jnp.bfloat16)
            aside()
        for number, (lo, hi) in enumerate(groups):
            for tile in range(lo, hi):
                columns = pl.ds(tile * OUT_TILE, OUT_TILE)
                result = jnp.dot(
                    act[...], down_w[:, columns], preferred_element_type=jnp.float32
                ).astype(jnp.bfloat16)
                part[places, :, :, columns] = result.reshape(CORES, nz, rows, OUT_TILE)
                aside()
            columns = group_columns[number]
            send(
                part.at[first + 1, :, :, columns],
                rs.at[first // 2, :, :, columns],
                rs_send.at[first // 2, number],
                rs_recv.at[first // 2, number],
                sibling,
            )
        while between:
            aside()

    def half_arrived(place):
        for number, columns in enumerate(group_columns):
            arrived(rs.at[place // 2, :, :, columns], rs_recv.at[place // 2, number])

    def f32(ref, *at):
        return ref[at].astype(jnp.float32)

    def both(place, at):
        return f32(part, place, *at) + f32(rs, place // 2, *at)

    def keep(place, at, value):
        part[place, *at] = value.astype(jnp.bfloat16)

    def sibling_rows(place):
        for k in range(nz):
            rows_arrived(place + 1, near[k])

    def later(action, *at):
        return functools.partial(action, *at)

    def sum_first(k):
        at = far[k]
        if k == 0:
            half_arrived(FIRST)
        keep(FIRST, (at,), both(FIRST, (at,)))
        send(part.at[FIRST, at], r1.at[0, at], r1_send.at[0, k], r1_recv.at[0, at], along_a)

    sibling_rows(OWN)
    for load in loads:
        load.wait()
    split = max(nz - 2, 0)
    asides = [later(pass_first, nz - 1)]
    asides += [later(pass_last, SECOND, k) for k in range(split, nz)]
    asides += [later(pass_last, DIAGONAL, k) for k in range(split)]
    experts_on(OWN, asides)
    sibling_rows(FIRST)
    experts_on(FIRST, [later(pass_last, DIAGONAL, k) for k in range(split, nz)])
    sibling_rows(SECOND)
    experts_on(SECOND, [lambda: None] + [later(sum_first, k) for k in range(nz)])
    sibling_rows(DIAGONAL)
    experts_on(DIAGONAL, [])
    def piece(k, columns):
        return (far[k], slice(None), columns)

    def sum_diagonal(g, k):
        at = piece(k, group_columns[g])
        keep(DIAGONAL, at, both(DIAGONAL, at))
        send(
            part.at[DIAGONAL, *at], r1.at[1, *at],
            r1_send.at[1 + g, k], r1_recv.at[1 + g, far[k]], along_a,
        )

    def sum_second(g, k):
        at = piece(k, group_columns[g])
        arrived(r1.at[1, *at], r1_recv.at[1 + g, far[k]])
        keep(SECOND, at, both(SECOND, at) + f32(r1, 1, *at))
        send(part.at[SECOND, *at], r2.at[at], r2_send.at[g, k], r2_recv.at[g, far[k]], along_b)

    def sum_own(g, k):
        at = piece(k, group_columns[g])
        if g == 0:
            arrived(r1.at[0, far[k]], r1_recv.at[0, far[k]])
        arrived(r2.at[at], r2_recv.at[g, far[k]])
        return both(OWN, at) + f32(r1, 0, *at) + f32(r2, *at)

    def along_z(g, k):
        columns = group_columns[g]
        at = piece(k, columns)

        def landed(number):
            place = (number, slice(None), columns)
            arrived(rz.at[place], rz_recv.at[g, number])
            return f32(rz, *place)

        value = sum_own(g, k)
        if k == nz - 1:
            for number in range(crossings, nz - 1):
                value += landed(number)
            out_ref[:, :, columns] = value.reshape(steps, tok_rows, value.shape[1]).astype(
                out_ref.dtype
            )
            return
        to = mate
        if k > crossings:
            value += landed(k - crossings - 1)
            to = far[k]
        keep(OWN, at, value)
        send(
            part.at[OWN, *at], rz.at[k, :, columns],
            rz_send.at[g, k], rz_recv.at[g, k], device(to, q, c),
        )

    half_arrived(OWN)
    half_arrived(SECOND)
    for g in range(len(groups)):
        columns = group_columns[g]
        arrived(rs.at[DIAGONAL // 2, :, :, columns], rs_recv.at[DIAGONAL // 2, g])
        for k in range(nz):
            sum_diagonal(g, k)
    parts = [(g, k) for g in range(len(groups)) for k in range(nz)]
    seconds = 0
    for g, k in [at for at in parts if at[1] < nz - 1] + [at for at in parts if at[1] == nz - 1]:
        while seconds < min(len(parts), g * nz + k + 2):
            sum_second(*parts[seconds])
            seconds += 1
        along_z(g, k)
    for copy in sends:
        copy.wait_send()


def fused(tokens, expert_ids, route_weight, gate_weight, up_weight, down_weight):
    device_count = lax.axis_size("ep")
    nz = device_count // (SQUARE * CORES)
    steps, tok_rows, features = tokens.shape
    hidden = gate_weight.shape[2]
    rows = steps * tok_rows
    group = nz * rows
    kind = tokens.dtype
    dma = pltpu.SemaphoreType.DMA
    vmem = pl.BlockSpec(memory_space=pltpu.VMEM)
    hbm = pl.BlockSpec(memory_space=pl.ANY)
    weight_bytes = 3 * features * hidden * 2
    return pl.pallas_call(
        functools.partial(fused_kernel, nz),
        out_shape=jax.ShapeDtypeStruct(tokens.shape, kind),
        in_specs=[hbm] * 6,
        out_specs=vmem,
        scratch_shapes=[
            pltpu.VMEM(tokens.shape, kind),
            pltpu.VMEM(expert_ids.shape, expert_ids.dtype),
            pltpu.VMEM(route_weight.shape, route_weight.dtype),
            pltpu.VMEM((features, hidden), kind),
            pltpu.VMEM((features, hidden), kind),
            pltpu.VMEM((hidden, features), kind),
            pltpu.VMEM((SQUARE * CORES, nz, rows, features + LANES), kind),
            pltpu.VMEM((CORES * group, hidden), kind),
            pltpu.VMEM((SQUARE * CORES, nz, rows, features), kind),
            pltpu.VMEM((SQUARE, nz, rows, features), kind),
            pltpu.VMEM((2, nz, rows, features), kind),
            pltpu.VMEM((nz, rows, features), kind),
            pltpu.VMEM((nz, rows, features), kind),
            dma((6,)),
            dma((SQUARE * CORES, nz)),
            dma((nz,)),
            dma((nz,)),
            dma((2, nz)),
            dma((SQUARE, nz)),
            dma((SQUARE, 2)),
            dma((SQUARE, 2)),
            dma((3, nz)),
            dma((3, nz)),
            dma((2, nz)),
            dma((2, nz)),
            dma((2, nz)),
            dma((2, nz)),
        ],
        compiler_params=pltpu.CompilerParams(
            collective_id=0, has_side_effects=True, vmem_limit_bytes=56 * 1024 * 1024
        ),
        cost_estimate=pl.CostEstimate(
            flops=2 * device_count * rows * 3 * features * hidden,
            bytes_accessed=weight_bytes,
            transcendentals=device_count * rows * hidden,
        ),
    )(tokens, expert_ids, route_weight, gate_weight, up_weight, down_weight)


def shards(tokens, expert_ids, route_weight, gate_weight, up_weight, down_weight):
    device_count = lax.axis_size("ep")
    expert_count = device_count // 2
    tok_rows = tokens.shape[1]
    features = tokens.shape[2]
    capacity = min(tok_rows, 2 * tok_rows * TOP // expert_count)
    every_row = capacity == tok_rows and device_count % (2 * SQUARE * CORES) == 0
    if every_row and STEPS * tok_rows % 16 == 0:
        return fused(tokens, expert_ids, route_weight, gate_weight, up_weight, down_weight)
    half_slots = capacity // 2
    gate_m = gate_weight[0]
    up_m = up_weight[0]
    down_m = down_weight[0]
    parity_odd = lax.axis_index("ep") % 2 == 1
    layouts = []
    outgoing = []
    for step_index in range(STEPS):
        slot_index, slot_source = slot_layout(expert_ids[step_index], expert_count, capacity)
        padded = jnp.concatenate(
            [tokens[step_index], jnp.zeros((1, features), tokens.dtype)], axis=0
        )
        blocks = padded[slot_source // TOP].reshape(expert_count, capacity, features)
        arrange_paired = blocks.reshape(expert_count, half_slots, 2, features)
        arrange_paired = jnp.where(parity_odd, arrange_paired[:, :, ::-1], arrange_paired)
        outgoing.append(
            arrange_paired.transpose(0, 2, 1, 3).reshape(device_count, half_slots, features)
        )
        layouts.append(slot_index)
    returned_list = []
    for sent in outgoing:
        received = lax.all_to_all(sent, "ep", split_axis=0, concat_axis=0, tiled=True)
        partner = partner_2(received, "ep", 0)
        width = received.shape[1]
        apply_received = jnp.concatenate([received, partner], axis=1)
        gate = jnp.einsum("scd,df->scf", apply_received, gate_m, preferred_element_type=jnp.float32)
        upper = jnp.einsum("scd,df->scf", apply_received, up_m, preferred_element_type=jnp.float32)
        act = (jax.nn.silu(gate) * upper).astype(jnp.bfloat16)
        parts = jnp.einsum("scf,fd->scd", act, down_m, preferred_element_type=jnp.float32).astype(
            jnp.bfloat16
        )
        back = partner_2(parts[:, width:], "ep", 0)
        summed = (parts[:, :width].astype(jnp.float32) + back.astype(jnp.float32)).astype(
            jnp.bfloat16
        )
        returned_list.append(lax.all_to_all(summed, "ep", split_axis=0, concat_axis=0, tiled=True))
    answers = []
    for step_index in range(STEPS):
        returned = returned_list[step_index]
        paired = returned.reshape(expert_count, 2, half_slots, features).transpose(0, 2, 1, 3)
        paired = jnp.where(parity_odd, paired[:, :, ::-1], paired)
        answers.append(paired.reshape(expert_count, capacity, features))
    outputs = []
    for step_index in range(STEPS):
        flattened = answers[step_index].reshape(expert_count * capacity, features)
        picked = flattened[layouts[step_index]].reshape(tok_rows, TOP, features)
        summed = jnp.sum(route_weight[step_index][:, :, None] * picked.astype(jnp.float32), axis=1)
        outputs.append(summed.astype(jnp.bfloat16))
    return jnp.stack(outputs)


def solution(mesh):
    in_specs = (
        P(None, ("groups", "ep"), None),
        P(None, ("groups", "ep"), None),
        P(None, ("groups", "ep"), None),
        P("ep", None, None),
        P("ep", None, None),
        P("ep", None, None),
    )
    out_specs = P(None, ("groups", "ep"), None)
    return jax.shard_map(shards, mesh=mesh, in_specs=in_specs, out_specs=out_specs, check_vma=False)
```

```python
import functools

import jax
import jax.numpy as jnp
from jax import lax
from jax.experimental import pallas as pl
from jax.experimental.pallas import tpu as pltpu
from jax.sharding import PartitionSpec as P

TOP = 8
STEPS = 2


def partner_2(block, axis, apart):
    count = lax.axis_size(axis)
    route = []
    for low in range(count):
        high = low | 1 << apart
        if high != low and high < count:
            route += [(low, high), (high, low)]
    return lax.ppermute(block, axis, route)


def slot_layout(block_ids, expert_count, capacity):
    pairs = block_ids.reshape(-1)
    count = pairs.shape[0]
    one_hot = (pairs[:, None] == jnp.arange(expert_count, dtype=jnp.int32)[None, :]).astype(
        jnp.float32
    )
    order = jnp.arange(count, dtype=jnp.int32)
    earlier = (order[None, :] < order[:, None]).astype(jnp.float32)
    before = jnp.dot(earlier, one_hot, precision=lax.Precision.HIGHEST)
    slot_rank = jnp.sum(before * one_hot, axis=1).astype(jnp.int32)
    slot_index = pairs * capacity + slot_rank
    slot_source = jnp.full((expert_count * capacity,), count, jnp.int32).at[slot_index].set(order)
    return (slot_index, slot_source)


LANES = 128
SQUARE = 4
CORES = 2
FF_TILE = 256
OUT_TILE = 512


OWN, FIRST, DIAGONAL, SECOND = 0, 2, 4, 6


def fused_kernel(
    nz, tok_ref, ids_ref, route_ref, gate_hbm, up_hbm, down_hbm, out_ref,
    gate_w, up_w, down_w, xg, act, part, rs, r1, r2, rz,
    w_sem, x_recv, x_send_z, x_send_a, x_send_b, x_send_s,
    rs_send, rs_recv, r1_send, r1_recv, r2_send, r2_recv, rz_send, rz_recv,
):
    steps, tok_rows, features = tok_ref.shape
    rows = steps * tok_rows
    hidden = act.shape[1]
    experts = nz * SQUARE
    me = lax.axis_index("ep")
    c = lax.rem(me, CORES)
    expert = lax.div(me, CORES)
    q = lax.rem(expert, SQUARE)
    z = lax.div(expert, SQUARE)
    x, y = lax.rem(q, 2), lax.div(q, 2)
    qx, qy = 2 * y + 1 - x, 2 * (1 - y) + x
    qa = qx * (1 - c) + qy * c
    qb = qy * (1 - c) + qx * c

    def device(to_z, to_q, to_c):
        return {"ep": (to_z * SQUARE + to_q) * CORES + to_c}

    sibling, along_a, along_b = device(z, q, 1 - c), device(z, qa, c), device(z, qb, c)
    mate = z + 1 - 2 * lax.rem(z, 2)
    across = [lax.rem(z + 2 * h, nz) for h in range(1, nz // 2)]
    near = [z, mate]
    for there in across:
        near += [there, there + mate - z]
    far = near[::-1]

    loads = [
        pltpu.make_async_copy(gate_hbm.at[0], gate_w, w_sem.at[0]),
        pltpu.make_async_copy(up_hbm.at[0], up_w, w_sem.at[1]),
        pltpu.make_async_copy(down_hbm.at[0], down_w, w_sem.at[2]),
    ]
    barrier = pltpu.get_barrier_semaphore()
    partners = [device(p, q, c) for p in [mate] + across] + [along_a, along_b, sibling]
    for partner in partners:
        pl.semaphore_signal(
            barrier, inc=1, device_id=partner, device_id_type=pl.DeviceIdType.MESH
        )
    for load in loads:
        load.start()

    xg[OWN, z, :, :features] = (
        tok_ref[...].astype(jnp.float32).reshape(rows, features).astype(jnp.bfloat16)
    )
    lane = lax.broadcasted_iota(jnp.int32, (rows, LANES), 1)
    lane_expert, lane_piece = lax.rem(lane, experts), lax.div(lane, experts)
    ids = ids_ref[...].reshape(rows, TOP)
    route = route_ref[...].reshape(rows, TOP)
    coef = jnp.zeros((rows, LANES), jnp.float32)
    for k in range(TOP):
        coef += jnp.where(ids[:, k : k + 1] == lane_expert, route[:, k : k + 1], 0.0)
    high = coef.astype(jnp.bfloat16).astype(jnp.float32)
    middle = (coef - high).astype(jnp.bfloat16).astype(jnp.float32)
    low = coef - high - middle
    pieces = jnp.where(
        lane_piece == 0,
        high,
        jnp.where(lane_piece == 1, middle, jnp.where(lane_piece == 2, low, 0.0)),
    )
    xg[OWN, z, :, features:] = pieces.astype(jnp.bfloat16)
    pl.semaphore_wait(barrier, len(partners))

    sends = []

    def send(src, dst, send_sem, recv_sem, to):
        copy = pltpu.make_async_remote_copy(
            src_ref=src,
            dst_ref=dst,
            send_sem=send_sem,
            recv_sem=recv_sem,
            device_id=to,
            device_id_type=pl.DeviceIdType.MESH,
        )
        copy.start()
        sends.append(copy)

    def arrived(dst, recv_sem):
        pltpu.make_async_remote_copy(
            src_ref=dst,
            dst_ref=dst,
            send_sem=x_send_s.at[0, 0],
            recv_sem=recv_sem,
            device_id=sibling,
            device_id_type=pl.DeviceIdType.MESH,
        ).wait_recv()

    def send_rows(place, at, there, send_sem, to):
        send(xg.at[place, at], xg.at[there, at], send_sem, x_recv.at[there, at], to)

    def rows_arrived(place, at):
        arrived(xg.at[place, at], x_recv.at[place, at])

    def pair(place, p):
        return xg.at[place, pl.ds(near[2 * p] - lax.rem(z, 2), 2)]

    def share(place, k):
        if k % 2 == 1:
            p = k // 2
            send(
                pair(place, p), pair(place + 1, p),
                x_send_s.at[place // 2, p], x_recv.at[place + 1, p], sibling,
            )

    def pass_own(k):
        send_rows(OWN, near[k], FIRST, x_send_a.at[k], along_a)
        send_rows(OWN, near[k], SECOND, x_send_b.at[0, k], along_b)
        share(OWN, k)

    def pass_first(k):
        rows_arrived(FIRST, near[k])
        send_rows(FIRST, near[k], DIAGONAL, x_send_b.at[1, k], along_b)
        share(FIRST, k)

    def pass_last(place, k):
        rows_arrived(place, near[k])
        share(place, k)

    for number, there in enumerate(across):
        send_rows(OWN, z, OWN, x_send_z.at[2 * number], device(there, q, c))
    send_rows(OWN, z, OWN, x_send_z.at[nz - 1], device(mate, q, c))
    pass_own(0)
    for k in range(1, nz):
        rows_arrived(OWN, near[k])
        if k % 2 == 0:
            send_rows(OWN, near[k], OWN, x_send_z.at[k - 1], device(mate, q, c))
        pass_own(k)
        pass_first(k - 1)
        if k >= 2:
            pass_last(SECOND, k - 2)

    tiles = features // OUT_TILE
    groups = [(0, tiles)]
    group_columns = [pl.ds(lo * OUT_TILE, (hi - lo) * OUT_TILE) for lo, hi in groups]

    def experts_on(first, between):
        between = list(between)

        def aside():
            if between:
                between.pop(0)()

        places = pl.ds(first, CORES)
        count = CORES * nz * rows
        tail = xg[places, :, :, features:].reshape(count, LANES).astype(jnp.float32)
        tail_lane = lax.broadcasted_iota(jnp.int32, tail.shape, 1)
        scale = jnp.sum(
            jnp.where(lax.rem(tail_lane, experts) == expert, tail, 0.0), axis=1, keepdims=True
        )
        for tile in range(hidden // FF_TILE):
            columns = pl.ds(tile * FF_TILE, FF_TILE)
            inputs = xg[places, :, :, :features].reshape(count, features)
            gate = jnp.dot(inputs, gate_w[:, columns], preferred_element_type=jnp.float32)
            upper = jnp.dot(inputs, up_w[:, columns], preferred_element_type=jnp.float32)
            silu = gate / (1.0 + jnp.exp(-gate))
            act[:, columns] = (scale * (silu * upper)).astype(jnp.bfloat16)
            aside()
        for number, (lo, hi) in enumerate(groups):
            for tile in range(lo, hi):
                columns = pl.ds(tile * OUT_TILE, OUT_TILE)
                result = jnp.dot(
                    act[...], down_w[:, columns], preferred_element_type=jnp.float32
                ).astype(jnp.bfloat16)
                part[places, :, :, columns] = result.reshape(CORES, nz, rows, OUT_TILE)
                aside()
            columns = group_columns[number]
            send(
                part.at[first + 1, :, :, columns],
                rs.at[first // 2, :, :, columns],
                rs_send.at[first // 2, number],
                rs_recv.at[first // 2, number],
                sibling,
            )
        while between:
            aside()

    def half_arrived(place):
        for number, columns in enumerate(group_columns):
            arrived(rs.at[place // 2, :, :, columns], rs_recv.at[place // 2, number])

    def f32(ref, *at):
        return ref[at].astype(jnp.float32)

    def both(place, at):
        return f32(part, place, at) + f32(rs, place // 2, at)

    def keep(place, at, value):
        part[place, at] = value.astype(jnp.bfloat16)

    def sibling_rows(place):
        for p in range(nz // 2):
            arrived(pair(place + 1, p), x_recv.at[place + 1, p])

    def later(action, *at):
        return functools.partial(action, *at)

    def sum_first(k):
        at = far[k]
        if k == 0:
            half_arrived(FIRST)
        keep(FIRST, at, both(FIRST, at))
        send(part.at[FIRST, at], r1.at[0, at], r1_send.at[0, k], r1_recv.at[0, at], along_a)

    sibling_rows(OWN)
    for load in loads:
        load.wait()
    split = max(nz - 2, 0)
    asides = [later(pass_first, nz - 1)]
    asides += [later(pass_last, SECOND, k) for k in range(split, nz)]
    asides += [later(pass_last, DIAGONAL, k) for k in range(split)]
    experts_on(OWN, asides)
    sibling_rows(FIRST)
    experts_on(FIRST, [later(pass_last, DIAGONAL, k) for k in range(split, nz)])
    sibling_rows(SECOND)
    experts_on(SECOND, [lambda: None] + [later(sum_first, k) for k in range(nz)])
    sibling_rows(DIAGONAL)
    experts_on(DIAGONAL, [])
    half_arrived(OWN)
    half_arrived(DIAGONAL)
    for k in range(nz):
        at = far[k]
        keep(DIAGONAL, at, both(DIAGONAL, at))
        send(part.at[DIAGONAL, at], r1.at[1, at], r1_send.at[1, k], r1_recv.at[1, at], along_a)
    half_arrived(SECOND)

    def sum_second(k):
        at = far[k]
        arrived(r1.at[1, at], r1_recv.at[1, at])
        keep(SECOND, at, both(SECOND, at) + f32(r1, 1, at))
        send(part.at[SECOND, at], r2.at[at], r2_send.at[k], r2_recv.at[at], along_b)

    def sum_own(k):
        at = far[k]
        arrived(r1.at[0, at], r1_recv.at[0, at])
        arrived(r2.at[at], r2_recv.at[at])
        return both(OWN, at) + f32(r1, 0, at) + f32(r2, at)

    sum_second(0)
    for k in range(nz - 1):
        sum_second(k + 1)
        at = far[k]
        value = sum_own(k)
        if k % 2 == 0:
            keep(OWN, at, value)
            send(part.at[OWN, at], rz.at[k], rz_send.at[k], rz_recv.at[k], device(mate, q, c))
        else:
            arrived(rz.at[k - 1], rz_recv.at[k - 1])
            keep(OWN, at, value + f32(rz, k - 1))
            send(part.at[OWN, at], rz.at[k], rz_send.at[k], rz_recv.at[k], device(at, q, c))
    total = sum_own(nz - 1)
    for k in list(range(1, nz - 1, 2)) + [nz - 2]:
        arrived(rz.at[k], rz_recv.at[k])
        total += f32(rz, k)
    out_ref[...] = total.reshape(steps, tok_rows, features).astype(out_ref.dtype)
    for copy in sends:
        copy.wait_send()


def fused(tokens, expert_ids, route_weight, gate_weight, up_weight, down_weight):
    device_count = lax.axis_size("ep")
    nz = device_count // (SQUARE * CORES)
    steps, tok_rows, features = tokens.shape
    hidden = gate_weight.shape[2]
    rows = steps * tok_rows
    group = nz * rows
    kind = tokens.dtype
    dma = pltpu.SemaphoreType.DMA
    vmem = pl.BlockSpec(memory_space=pltpu.VMEM)
    hbm = pl.BlockSpec(memory_space=pl.ANY)
    weight_bytes = 3 * features * hidden * 2
    return pl.pallas_call(
        functools.partial(fused_kernel, nz),
        out_shape=jax.ShapeDtypeStruct(tokens.shape, kind),
        in_specs=[vmem, vmem, vmem, hbm, hbm, hbm],
        out_specs=vmem,
        scratch_shapes=[
            pltpu.VMEM((features, hidden), kind),
            pltpu.VMEM((features, hidden), kind),
            pltpu.VMEM((hidden, features), kind),
            pltpu.VMEM((SQUARE * CORES, nz, rows, features + LANES), kind),
            pltpu.VMEM((CORES * group, hidden), kind),
            pltpu.VMEM((SQUARE * CORES, nz, rows, features), kind),
            pltpu.VMEM((SQUARE, nz, rows, features), kind),
            pltpu.VMEM((2, nz, rows, features), kind),
            pltpu.VMEM((nz, rows, features), kind),
            pltpu.VMEM((nz, rows, features), kind),
            dma((3,)),
            dma((SQUARE * CORES, nz)),
            dma((nz,)),
            dma((nz,)),
            dma((2, nz)),
            dma((SQUARE, nz)),
            dma((SQUARE, 2)),
            dma((SQUARE, 2)),
            dma((2, nz)),
            dma((2, nz)),
            dma((nz,)),
            dma((nz,)),
            dma((nz,)),
            dma((nz,)),
        ],
        compiler_params=pltpu.CompilerParams(
            collective_id=0, has_side_effects=True, vmem_limit_bytes=56 * 1024 * 1024
        ),
        cost_estimate=pl.CostEstimate(
            flops=2 * device_count * rows * 3 * features * hidden,
            bytes_accessed=weight_bytes,
            transcendentals=device_count * rows * hidden,
        ),
    )(tokens, expert_ids, route_weight, gate_weight, up_weight, down_weight)


def shards(tokens, expert_ids, route_weight, gate_weight, up_weight, down_weight):
    device_count = lax.axis_size("ep")
    expert_count = device_count // 2
    tok_rows = tokens.shape[1]
    features = tokens.shape[2]
    capacity = min(tok_rows, 2 * tok_rows * TOP // expert_count)
    every_row = capacity == tok_rows and device_count % (2 * SQUARE * CORES) == 0
    if every_row and STEPS * tok_rows % 16 == 0:
        return fused(tokens, expert_ids, route_weight, gate_weight, up_weight, down_weight)
    half_slots = capacity // 2
    gate_m = gate_weight[0]
    up_m = up_weight[0]
    down_m = down_weight[0]
    parity_odd = lax.axis_index("ep") % 2 == 1
    layouts = []
    outgoing = []
    for step_index in range(STEPS):
        slot_index, slot_source = slot_layout(expert_ids[step_index], expert_count, capacity)
        padded = jnp.concatenate(
            [tokens[step_index], jnp.zeros((1, features), tokens.dtype)], axis=0
        )
        blocks = padded[slot_source // TOP].reshape(expert_count, capacity, features)
        arrange_paired = blocks.reshape(expert_count, half_slots, 2, features)
        arrange_paired = jnp.where(parity_odd, arrange_paired[:, :, ::-1], arrange_paired)
        outgoing.append(
            arrange_paired.transpose(0, 2, 1, 3).reshape(device_count, half_slots, features)
        )
        layouts.append(slot_index)
    returned_list = []
    for sent in outgoing:
        received = lax.all_to_all(sent, "ep", split_axis=0, concat_axis=0, tiled=True)
        partner = partner_2(received, "ep", 0)
        width = received.shape[1]
        apply_received = jnp.concatenate([received, partner], axis=1)
        gate = jnp.einsum("scd,df->scf", apply_received, gate_m, preferred_element_type=jnp.float32)
        upper = jnp.einsum("scd,df->scf", apply_received, up_m, preferred_element_type=jnp.float32)
        act = (jax.nn.silu(gate) * upper).astype(jnp.bfloat16)
        parts = jnp.einsum("scf,fd->scd", act, down_m, preferred_element_type=jnp.float32).astype(
            jnp.bfloat16
        )
        back = partner_2(parts[:, width:], "ep", 0)
        summed = (parts[:, :width].astype(jnp.float32) + back.astype(jnp.float32)).astype(
            jnp.bfloat16
        )
        returned_list.append(lax.all_to_all(summed, "ep", split_axis=0, concat_axis=0, tiled=True))
    answers = []
    for step_index in range(STEPS):
        returned = returned_list[step_index]
        paired = returned.reshape(expert_count, 2, half_slots, features).transpose(0, 2, 1, 3)
        paired = jnp.where(parity_odd, paired[:, :, ::-1], paired)
        answers.append(paired.reshape(expert_count, capacity, features))
    outputs = []
    for step_index in range(STEPS):
        flattened = answers[step_index].reshape(expert_count * capacity, features)
        picked = flattened[layouts[step_index]].reshape(tok_rows, TOP, features)
        summed = jnp.sum(route_weight[step_index][:, :, None] * picked.astype(jnp.float32), axis=1)
        outputs.append(summed.astype(jnp.bfloat16))
    return jnp.stack(outputs)


def solution(mesh):
    in_specs = (
        P(None, ("groups", "ep"), None),
        P(None, ("groups", "ep"), None),
        P(None, ("groups", "ep"), None),
        P("ep", None, None),
        P("ep", None, None),
        P("ep", None, None),
    )
    out_specs = P(None, ("groups", "ep"), None)
    return jax.shard_map(shards, mesh=mesh, in_specs=in_specs, out_specs=out_specs, check_vma=False)
```
